32 devices in a mesh: grp: 4 (over x, core), row: 8 (over z, y).
Axes of the slice: x: 2, y: 2, z: 4, core: 2. Of those that a mesh axis runs over, the one named last changes fastest.
Arguments:
- surface: float32 [16384, 256], P(('grp', 'row')), may hold values from -6 to 6
- panel_lower: bfloat16 [16384, 1024], P(('grp', 'row')), may hold values from -0.1875 to 0.1875
- top_rows: bfloat16 [1024, 256], P('row'), may hold values from -6 to 6
- panel_inverse: bfloat16 [1024, 1024], P('row'), may hold values from -0.1875 to 0.1875
- panel_order: int32 [1024], replicated, may hold values from 0 to 1023, each once
- front_inverse: bfloat16 [4, 6144, 6144], P('grp', 'row'), may hold values from -0.078125 to 0.078125
- front_upper: bfloat16 [4, 6144, 256], P('grp', 'row'), may hold values from -6 to 6
- front_lower: bfloat16 [4, 1024, 6144], P('grp', None, 'row'), may hold values from -0.078125 to 0.078125
- front_sizes: int32 [4], replicated, may hold values from 1536 to 6144, as said below
- border_blocks: int32 [4, 8], replicated, may hold values from 0 to 127
Outputs:
- updated: float32 [16384, 256], P(('grp', 'row'))
The draws below stay inside these ranges and needn't reach their ends.
Inputs may be any that keep to these rules, and one draw needn't show every extreme that they name: `front_sizes`: every front has at least 1536 live pivots, and in every draw some front has exactly 6144.
All inputs are finite; a program needn't handle non-finite values.
Results may differ from the reference program's by a relative error of at most 0.0022.
Values may be sent and summed in bfloat16 or wider, within the bound.
No kernel may reach another device: no remote copies, remote signals or barrier semaphores. Data moves between devices by JAX's collectives and lax.ppermute only.
A program may use at most 64 MiB of HBM per device.

```python
import jax
import jax.numpy as jnp
from jax import lax

COLS = 256
PIV = 6144
BORDER = 1024
PANEL = 1024
BLOCK = 128
ROWS_DEV = 512
FRONTS = 4
BBLK = 8
ROWS = 16384
RBLK = 128
N_GRP = 4
N_ROW = 8


def draw_front_sizes(key, part):
    size_key = jax.random.fold_in(key, 11)
    pick_key = jax.random.fold_in(key, 23)
    sizes = jax.random.randint(size_key, (FRONTS,), PIV // 4, PIV + 1)
    fullest = jax.random.randint(pick_key, (), 0, FRONTS)
    return jnp.where(jnp.arange(FRONTS) == fullest, PIV, sizes).astype(jnp.int32)


def draw_border_blocks(key, part):
    base_key = jax.random.fold_in(key, 31)
    which_key = jax.random.fold_in(key, 37)
    local_key = jax.random.fold_in(key, 41)
    uniform_targets = jax.random.randint(base_key, (FRONTS, BBLK), 0, RBLK)
    chosen = jax.random.randint(which_key, (FRONTS,), 0, BBLK)
    local_pick = jax.random.randint(local_key, (FRONTS,), 0, ROWS_DEV // BLOCK)
    device_total = N_GRP * N_ROW
    share = BORDER // N_ROW
    front_ids = jnp.arange(FRONTS, dtype=jnp.int32)
    source_device = front_ids * N_ROW + chosen * BLOCK // share
    far_device = (source_device + device_total // 2) % device_total
    forced = far_device * (ROWS_DEV // BLOCK) + local_pick
    slot_ids = jnp.arange(BBLK, dtype=jnp.int32)
    result = jnp.where(slot_ids[None, :] == chosen[:, None], forced[:, None], uniform_targets)
    return result.astype(jnp.int32)


def block_levels(key, extent, pieces, least, top_value):
    factor_of = 1.0
    for dim, parts in pieces:
        draws = jax.random.uniform(jax.random.fold_in(jax.random.fold_in(key, 6), dim), (parts,), jnp.float32, least / len(pieces), top_value / len(pieces))
        factor_of = factor_of * jnp.repeat(jnp.exp(draws), extent[dim] // parts).reshape((-1,) + (1,) * (len(extent) - 1 - dim))
    return factor_of


def centred(own_key, extent, scale, bound, shards=(), kind=jnp.bfloat16):
    level = block_levels(own_key, extent, shards, -0.22, 0.18) if shards else 1.0
    drawn = jax.random.normal(own_key, extent, jnp.float32) * scale * level
    return jnp.minimum(jnp.maximum(drawn, -bound), bound).astype(kind)


def setup_inputs(seed: int = 0) -> dict:
    key_list = jax.random.split(jax.random.key(seed), 11)
    return {
        "surface": centred(key_list[0], (ROWS, COLS), 1.0, 6.0, ((0, 32),), jnp.float32),
        "panel_lower": centred(key_list[1], (ROWS, PANEL), PANEL ** -0.5, 0.1875, ((0, 32),)),
        "top_rows": centred(key_list[2], (PANEL, COLS), 1.0, 6.0, ((0, 8),)),
        "panel_inverse": centred(key_list[3], (PANEL, PANEL), PANEL ** -0.5, 0.1875, ((0, 8),)),
        "panel_order": jax.random.permutation(key_list[4], PANEL).astype(jnp.int32),
        "front_inverse": centred(key_list[5], (FRONTS, PIV, PIV), PIV ** -0.5, 0.078125, ((0, 4), (1, 8))),
        "front_upper": centred(key_list[6], (FRONTS, PIV, COLS), 1.0, 6.0, ((0, 4), (1, 8))),
        "front_lower": centred(key_list[7], (FRONTS, BORDER, PIV), PIV ** -0.5, 0.078125, ((0, 4), (2, 8))),
        "front_sizes": draw_front_sizes(jax.random.fold_in(key_list[10], 71), 0),
        "border_blocks": draw_border_blocks(jax.random.fold_in(key_list[10], 71), 0),
    }


def one_front(operands):
    inverse, upper, lower = operands
    solved = jnp.dot(inverse, upper, preferred_element_type=jnp.float32).astype(jnp.bfloat16)
    return jnp.dot(lower, solved, preferred_element_type=jnp.float32)


def reference(surface, panel_lower, top_rows, panel_inverse, panel_order, front_inverse, front_upper, front_lower, front_sizes, border_blocks):
    pivot_ids = jnp.arange(PIV, dtype=jnp.int32)
    live_mask = pivot_ids[None, :] < front_sizes[:, None]
    upper_kept = jnp.where(live_mask[:, :, None], front_upper, jnp.zeros_like(front_upper))
    lower_kept = jnp.where(live_mask[:, None, :], front_lower, jnp.zeros_like(front_lower))
    contribution = lax.map(one_front, (front_inverse, upper_kept, lower_kept))
    col_count = surface.shape[1]
    slabs = contribution.reshape(FRONTS * BBLK, BLOCK * col_count)
    targets = border_blocks.reshape(-1).astype(jnp.int32)
    block_ids = jnp.arange(RBLK, dtype=jnp.int32)
    selector = (block_ids[:, None] == targets[None, :]).astype(jnp.float32)
    collected = jnp.dot(selector, slabs, precision=lax.Precision.HIGHEST, preferred_element_type=jnp.float32)
    collected = collected.reshape(surface.shape)
    ordered = jnp.take(top_rows, panel_order.astype(jnp.int32), axis=0)
    panel_ids = jnp.arange(PANEL, dtype=jnp.int32)
    strict = jnp.where(panel_ids[None, :] < panel_ids[:, None], panel_inverse, jnp.zeros_like(panel_inverse))
    factor = (jnp.dot(strict, ordered, preferred_element_type=jnp.float32) + ordered.astype(jnp.float32)).astype(jnp.bfloat16)
    return surface - collected - jnp.dot(panel_lower, factor, preferred_element_type=jnp.float32)
```

```python
import functools

import jax
import jax.numpy as jnp
from jax import lax
from jax.experimental import pallas as pl
from jax.experimental.pallas import tpu as pltpu
from jax.sharding import PartitionSpec as P

BLOCK = 128
HALVES = 2
NEXT = (1, 3, 0, 2)
PREV = (2, 0, 3, 1)
LIMIT = 40 << 20
F32 = jnp.float32
BF16 = jnp.bfloat16
together = lax.optimization_barrier


def params():
    return pltpu.CompilerParams(vmem_limit_bytes=LIMIT)


def whole(shape):
    return pl.BlockSpec(shape, lambda *_: (0,) * len(shape))


def row_permute(value, target):
    pairs = [(z * 2 + y, target(z, y)) for z in range(4) for y in range(2)]
    return lax.ppermute(value, "row", [(s, t[0] * 2 + t[1]) for s, t in pairs])


def cycle(value):
    return row_permute(value, lambda z, y: (NEXT[z], y))


def across(value):
    return row_permute(value, lambda z, y: (z, 1 - y))


def along(value, step):
    return row_permute(value, lambda z, y: (z ^ step, y))


def group_swap(value, step):
    return lax.ppermute(value, "grp", [(g, g ^ step) for g in range(4)])


def multiply_body(count, has_total, blocks_ref, inverse_ref, *refs):
    pieces = refs[:count]
    total_ref = refs[-1]
    step = pl.program_id(0)
    for k in range(count):

        @pl.when(step == k)
        def _():
            part = jnp.dot(inverse_ref[...], pieces[k][...], preferred_element_type=F32)
            if k > 0:
                total_ref[...] += part
            elif has_total:
                total_ref[...] = refs[count][...] + part
            else:
                total_ref[...] = part


def multiply(inverse, blocks, pieces, total=None):
    rows = inverse.shape[0]
    depth, cols = pieces[0].shape
    count = len(pieces)
    extra = [] if total is None else [total]
    return pl.pallas_call(
        functools.partial(multiply_body, count, bool(extra)),
        out_shape=jax.ShapeDtypeStruct((rows, cols), F32),
        grid_spec=pltpu.PrefetchScalarGridSpec(
            num_scalar_prefetch=1,
            grid=(count,),
            in_specs=[pl.BlockSpec((rows, depth), lambda i, b: (0, b[i]))]
            + [whole((depth, cols))] * count
            + [whole((rows, cols))] * len(extra),
            out_specs=whole((rows, cols)),
        ),
        compiler_params=params(),
        cost_estimate=pl.CostEstimate(
            flops=2 * rows * depth * cols * count,
            bytes_accessed=2 * rows * depth * count,
            transcendentals=0,
        ),
    )(blocks, inverse, *pieces, *extra)


def contribute_body(count, scalars_ref, inverse_ref, *refs):
    pieces = refs[:count]
    before_ref, lower_ref, keep_ref, send_ref, total_ref, product_ref = refs[count:]
    step = pl.program_id(0)
    for k in range(count):

        @pl.when(step == k)
        def _():
            part = jnp.dot(inverse_ref[...], pieces[k][...], preferred_element_type=F32)
            total_ref[...] = (before_ref if k == 0 else total_ref)[...] + part

    @pl.when(step == count - 1)
    def _():
        live, own_y = scalars_ref[count], scalars_ref[count + 1]
        pivots = lax.broadcasted_iota(jnp.int32, total_ref.shape, 0)
        solved = jnp.where(pivots < live, total_ref[...], 0.0).astype(BF16)
        product_ref[...] = jnp.dot(lower_ref[...], solved, preferred_element_type=F32)
        slots, slabs, height, _ = keep_ref.shape
        for z in range(slots):
            for j in range(slabs):
                base = j * BLOCK + z * 2 * height
                mine = pl.multiple_of(base + own_y * height, height)
                other = pl.multiple_of(base + (1 - own_y) * height, height)
                keep_ref[z, j] = product_ref[pl.ds(mine, height)]
                send_ref[z, j] = product_ref[pl.ds(other, height)].astype(BF16)


def contribute(inverse, scalars, pieces, before, lower):
    rows = inverse.shape[0]
    depth, cols = pieces[0].shape
    border = lower.shape[0]
    count = len(pieces)
    slots = (4, border // BLOCK, BLOCK // 8, cols)
    return pl.pallas_call(
        functools.partial(contribute_body, count),
        out_shape=[jax.ShapeDtypeStruct(slots, F32), jax.ShapeDtypeStruct(slots, BF16)],
        grid_spec=pltpu.PrefetchScalarGridSpec(
            num_scalar_prefetch=1,
            grid=(count,),
            in_specs=[pl.BlockSpec((rows, depth), lambda i, b: (0, b[i]))]
            + [whole((depth, cols))] * count
            + [whole((rows, cols)), whole((border, rows))],
            out_specs=[whole(slots), whole(slots)],
            scratch_shapes=[pltpu.VMEM((rows, cols), F32), pltpu.VMEM((border, cols), F32)],
        ),
        compiler_params=params(),
        cost_estimate=pl.CostEstimate(
            flops=2 * rows * cols * (depth * count + border),
            bytes_accessed=2 * rows * (depth * count + border),
            transcendentals=0,
        ),
    )(scalars, inverse, *pieces, before, lower)


def split_body(z_ref, keep_ref, come_ref, own_ref, *send_refs):
    z = z_ref[0]
    own_ref[...] = keep_ref[z] + come_ref[z].astype(F32)
    for k, ref in enumerate(send_refs, 1):
        ref[...] = (keep_ref[z ^ k] + come_ref[z ^ k].astype(F32)).astype(BF16)


def split(z, keep, come):
    shape = keep.shape[1:]
    return pl.pallas_call(
        split_body,
        out_shape=[jax.ShapeDtypeStruct(shape, F32)] + [jax.ShapeDtypeStruct(shape, BF16)] * 3,
        in_specs=[pl.BlockSpec(memory_space=pltpu.SMEM)]
        + [pl.BlockSpec(memory_space=pltpu.VMEM)] * 2,
        out_specs=[pl.BlockSpec(memory_space=pltpu.VMEM)] * 4,
        compiler_params=params(),
    )(z[None], keep, come)


def place_body(targets_ref, first_ref, *refs):
    pieces, slots_ref, total_ref = refs[:4], refs[4], refs[5]
    total_ref[...] = jnp.zeros_like(total_ref)
    blocks = total_ref.shape[0]
    slabs = pieces[0].shape[0]
    first, group = first_ref[0], first_ref[1]
    for k, piece in enumerate(pieces):
        for j in range(slabs):
            place = targets_ref[group ^ k, j] - first

            @pl.when((place >= 0) & (place < blocks))
            def _():
                total_ref[place] += piece[j].astype(F32)

    slots_ref[...] = total_ref[...].astype(BF16)


def place(targets, first, pieces, blocks):
    shape = (blocks,) + pieces[0].shape[1:]
    return pl.pallas_call(
        place_body,
        out_shape=jax.ShapeDtypeStruct(shape, BF16),
        in_specs=[pl.BlockSpec(memory_space=pltpu.SMEM)] * 2
        + [pl.BlockSpec(memory_space=pltpu.VMEM)] * 4,
        out_specs=pl.BlockSpec(memory_space=pltpu.VMEM),
        scratch_shapes=[pltpu.VMEM(shape, F32)],
        compiler_params=params(),
    )(targets, first, *pieces)


def factor_body(place_ref, order_ref, inverse_ref, mine_ref, other_ref, out_ref):
    row, core = place_ref[0], place_ref[1]
    local, width = inverse_ref.shape
    half = local // 2
    rows = row * local + lax.broadcasted_iota(jnp.int32, (local, width), 0)
    cols = lax.broadcasted_iota(jnp.int32, (local, width), 1)
    lower = jnp.where(cols < rows, inverse_ref[...].astype(F32), jnp.where(cols == rows, 1.0, 0.0))
    lower = lower.astype(BF16)
    total = jnp.zeros((local, out_ref.shape[1]), F32)
    for ref, side in ((mine_ref, core), (other_ref, 1 - core)):
        for k in range(width // local):
            first = (row ^ k) * local + side * half
            ids = first + lax.broadcasted_iota(jnp.int32, (half, width), 0)
            pick = (ids == order_ref[...]).astype(F32).astype(BF16)
            moved = lax.dot_general(
                lower, pick, (((1,), (1,)), ((), ())), preferred_element_type=F32
            ).astype(BF16)
            total += jnp.dot(moved, ref[k], preferred_element_type=F32)
    out_ref[...] = total.astype(BF16)


def panel_factor(place_scalars, order, inverse, mine, other):
    local = inverse.shape[0]
    return pl.pallas_call(
        factor_body,
        out_shape=jax.ShapeDtypeStruct((local, mine.shape[-1]), BF16),
        in_specs=[pl.BlockSpec(memory_space=pltpu.SMEM)]
        + [pl.BlockSpec(memory_space=pltpu.VMEM)] * 4,
        out_specs=pl.BlockSpec(memory_space=pltpu.VMEM),
        compiler_params=params(),
    )(place_scalars, order[None], inverse, mine, other)


def base_body(place_ref, surface_ref, lower_ref, mine_ref, other_ref, out_ref, factor_ref):
    row, core = place_ref[0], place_ref[1]
    half = mine_ref.shape[1]
    for ref, side in ((mine_ref, core), (other_ref, 1 - core)):
        for k in range(mine_ref.shape[0]):
            first = pl.multiple_of(((row ^ k) * 2 + side) * half, half)
            factor_ref[pl.ds(first, half)] = ref[k]
    product = jnp.dot(lower_ref[...], factor_ref[...], preferred_element_type=F32)
    out_ref[...] = surface_ref[...] - product


def panel_update(place_scalars, surface, lower, mine, other):
    return pl.pallas_call(
        base_body,
        out_shape=jax.ShapeDtypeStruct(surface.shape, F32),
        in_specs=[pl.BlockSpec(memory_space=pltpu.SMEM)]
        + [pl.BlockSpec(memory_space=pltpu.VMEM)] * 4,
        out_specs=pl.BlockSpec(memory_space=pltpu.VMEM),
        scratch_shapes=[pltpu.VMEM((lower.shape[1], surface.shape[1]), BF16)],
        compiler_params=params(),
    )(place_scalars, surface, lower, mine, other)


def doubled(value):
    pair = jnp.stack([value, across(value)])
    four = jnp.concatenate([pair, along(pair, 1)])
    return jnp.concatenate([four, along(four, 2)])


def staged(
    surface,
    panel_lower,
    top_rows,
    panel_inverse,
    panel_order,
    front_inverse,
    front_upper,
    front_lower,
    front_sizes,
    border_blocks,
):
    row_count = lax.axis_size("row")
    group = lax.axis_index("grp")
    row = lax.axis_index("row")
    z, y, core = row // 2, row % 2, group % 2
    inverse, upper, lower = front_inverse[0], front_upper[0], front_lower[0]
    local_piv = upper.shape[0]
    live = front_sizes[group] - row * local_piv
    kept = jnp.where(jnp.arange(local_piv, dtype=jnp.int32)[:, None] < live, upper, 0)
    depth = local_piv // HALVES
    a, b = kept[:depth], kept[depth:]
    spot = jnp.stack([row, core])

    half = top_rows.shape[0] // 2
    top_half = lax.dynamic_slice_in_dim(top_rows, core * half, half, 0)
    top_mine = doubled(top_half)
    top_other = group_swap(top_mine, 1)
    own_factor = panel_factor(spot, panel_order, panel_inverse, top_mine, top_other)
    factor_half = lax.dynamic_slice_in_dim(own_factor, core * half, half, 0)
    factor_mine = doubled(factor_half)
    factor_other = group_swap(factor_mine, 1)
    base = panel_update(spot, surface, panel_lower, factor_mine, factor_other)

    a1, ay0, b1, by0 = cycle(a), across(a), cycle(b), across(b)
    a1, ay0 = together((a1, ay0))
    a2, ay1 = cycle(a1), across(a1)
    b1, by0 = together((b1, by0))
    b2, by1 = cycle(b1), across(b1)
    a2, ay1 = together((a2, ay1))
    a3, ay2 = cycle(a2), across(a2)
    b2, by1 = together((b2, by1))
    b3, by2 = cycle(b2), across(b2)
    a3, ay2 = together((a3, ay2))
    ay3 = across(a3)
    b3, by2 = together((b3, by2))
    by3 = across(b3)

    prev = jnp.asarray(PREV, jnp.int32)
    sources = [z]
    for _ in range(3):
        sources.append(prev[sources[-1]])

    def block(k, other, h):
        return (sources[k] * 2 + (1 - y if other else y)) * HALVES + h

    early = [(0, 0, 0, a), (0, 0, 1, b), (1, 0, 0, a1), (0, 1, 0, ay0), (1, 0, 1, b1)]
    early += [(0, 1, 1, by0), (2, 0, 0, a2), (1, 1, 0, ay1), (2, 0, 1, b2), (1, 1, 1, by1)]
    late = [(3, 0, 0, a3), (2, 1, 0, ay2), (3, 0, 1, b3), (2, 1, 1, by2)]
    late += [(3, 1, 0, ay3), (3, 1, 1, by3)]
    early_blocks = jnp.stack([block(*e[:3]) for e in early])
    late_scalars = jnp.stack([block(*e[:3]) for e in late] + [live, y])
    total = multiply(inverse, early_blocks, [e[3] for e in early])
    keep, send = contribute(inverse, late_scalars, [e[3] for e in late], total, lower)

    own, s1, s2, s3 = split(z, keep, across(send))
    r3, r2, r1 = along(s3, 3), along(s2, 2), along(s1, 1)
    mine = (own + r1.astype(F32) + r2.astype(F32) + r3.astype(F32)).astype(BF16)
    pieces = [mine] + [group_swap(mine, k) for k in (1, 2, 3)]
    local_blocks = surface.shape[0] // BLOCK
    blocks = local_blocks * row_count
    slots = place(border_blocks, jnp.stack([group * blocks, group]), pieces, blocks)
    slots = slots.reshape((row_count, local_blocks) + slots.shape[1:])
    got = lax.all_to_all(slots, "row", 0, 0, tiled=True)
    collected = got.transpose(1, 0, 2, 3).reshape(surface.shape).astype(F32)
    return base - collected


def gathered(
    surface,
    panel_lower,
    top_rows,
    panel_inverse,
    panel_order,
    front_inverse,
    front_upper,
    front_lower,
    front_sizes,
    border_blocks,
):
    row_count = lax.axis_size("row")
    grp_index = lax.axis_index("grp")
    row_index = lax.axis_index("row")
    inverse_rows, upper_local, lower_local = front_inverse[0], front_upper[0], front_lower[0]
    local_piv, col_count = upper_local.shape
    pivot_ids = row_index * local_piv + jnp.arange(local_piv, dtype=jnp.int32)
    live_mask = pivot_ids < front_sizes[grp_index]
    upper_kept = jnp.where(live_mask[:, None], upper_local, jnp.zeros_like(upper_local))
    lower_kept = jnp.where(live_mask[None, :], lower_local, jnp.zeros_like(lower_local))
    upper_all = lax.all_gather(upper_kept, "row", axis=0, tiled=True)
    solved = jnp.dot(inverse_rows, upper_all, preferred_element_type=F32).astype(BF16)
    partial_sum = jnp.dot(lower_kept, solved, preferred_element_type=F32)
    own_share = lax.psum_scatter(partial_sum, "row", scatter_dimension=0, tiled=True)
    contributions = lax.all_gather(own_share, ("grp", "row"), axis=0, tiled=True)
    local_blocks = surface.shape[0] // BLOCK
    device_id = grp_index * row_count + row_index
    own_ids = device_id * local_blocks + jnp.arange(local_blocks, dtype=jnp.int32)
    targets = border_blocks.reshape(-1)
    selector = (own_ids[:, None] == targets[None, :]).astype(F32)
    slabs = contributions.reshape(targets.shape[0], BLOCK * col_count)
    collected = jnp.dot(
        selector, slabs, precision=lax.Precision.HIGHEST, preferred_element_type=F32
    ).reshape(surface.shape)
    local_panel, panel_width = panel_inverse.shape
    panel_ids = jnp.arange(panel_width, dtype=jnp.int32)
    top_all = lax.all_gather(top_rows, "row", axis=0, tiled=True)
    ordered = jnp.take(top_all, panel_order, axis=0)
    own_rows = row_index * local_panel + jnp.arange(local_panel, dtype=jnp.int32)
    strict = jnp.where(
        panel_ids[None, :] < own_rows[:, None], panel_inverse, jnp.zeros_like(panel_inverse)
    )
    own_top = lax.dynamic_slice_in_dim(ordered, row_index * local_panel, local_panel, 0)
    product = jnp.dot(strict, ordered, preferred_element_type=F32)
    own_solved = (product + own_top.astype(F32)).astype(BF16)
    factor = lax.all_gather(own_solved, "row", axis=0, tiled=True)
    return surface - collected - jnp.dot(panel_lower, factor, preferred_element_type=F32)


def solution(mesh):
    in_specs = (
        P(("grp", "row"), None),
        P(("grp", "row"), None),
        P("row", None),
        P("row", None),
        P(),
        P("grp", "row", None),
        P("grp", "row", None),
        P("grp", None, "row"),
        P(),
        P(),
    )
    out_specs = P(("grp", "row"), None)
    small = mesh.shape["row"] == 8 and mesh.shape["grp"] == 4
    return jax.shard_map(
        staged if small else gathered,
        mesh=mesh,
        in_specs=in_specs,
        out_specs=out_specs,
        check_vma=False,
    )
```

```python
import functools

import jax
import jax.numpy as jnp
from jax import lax
from jax.experimental import pallas as pl
from jax.experimental.pallas import tpu as pltpu
from jax.sharding import PartitionSpec as P

BLOCK = 128
PARTS = 2
NEXT = (1, 3, 0, 2)
LIMIT = 20 << 20
F32 = jnp.float32
BF16 = jnp.bfloat16
together = lax.optimization_barrier


def params():
    return pltpu.CompilerParams(vmem_limit_bytes=LIMIT)


def row_permute(value, target):
    pairs = [(z * 2 + y, target(z, y)) for z in range(4) for y in range(2)]
    return lax.ppermute(value, "row", [(s, t[0] * 2 + t[1]) for s, t in pairs])


def cycle(value):
    return row_permute(value, lambda z, y: (NEXT[z], y))


def across(value):
    return row_permute(value, lambda z, y: (z, 1 - y))


def along(value, step):
    return row_permute(value, lambda z, y: (z ^ step, y))


def group_swap(value, step):
    return lax.ppermute(value, "grp", [(g, g ^ step) for g in range(4)])


def before(place):
    return (place >> 1) | ((1 - (place & 1)) << 1)


SMEM = pl.BlockSpec(memory_space=pltpu.SMEM)
VMEM = pl.BlockSpec(memory_space=pltpu.VMEM)
HBM = pl.BlockSpec(memory_space=pltpu.HBM)


def source_rows(spot_ref, steps, crossed):
    row = spot_ref[0]
    spot = row // 2
    for _ in range(steps):
        spot = before(spot)
    return spot * 2 + ((row & 1) ^ crossed)


def live_rows(piece, first, live):
    ids = lax.broadcasted_iota(jnp.int32, piece.shape, 0)
    return jnp.where(ids < live - first, piece.astype(F32), 0.0).astype(BF16)


def multiply_body(names, spot_ref, sizes_ref, inverse_ref, *refs):
    pieces = refs[: len(names)]
    total_ref, later_ref, left, right, sem = refs[len(names) :]
    chunks, height, _ = left.shape
    copies = [
        pltpu.make_async_copy(inverse_ref.at[pl.ds(c * height, height)], left.at[c], sem.at[c])
        for c in range(chunks)
    ]
    for copy in copies:
        copy.start()
    live = sizes_ref[spot_ref[1]]
    width, cols = right.shape
    share = later_ref.shape[1]
    depth = share // PARTS
    for (steps, crossed, part), piece in zip(names, pieces):
        source = source_rows(spot_ref, steps, crossed)
        first = pl.multiple_of((source * PARTS + part) * depth, depth)
        right[pl.ds(first, depth)] = live_rows(piece[:depth], first, live)
    late = pl.multiple_of(source_rows(spot_ref, 3, 1) * share, share)
    right[pl.ds(late, share)] = jnp.zeros((share, cols), BF16)
    for c in range(chunks):
        copies[c].wait()
        rows = pl.ds(c * height, height)
        total_ref[rows] = jnp.dot(left[c], right[...], preferred_element_type=F32)
        later_ref[rows] = left[c, :, pl.ds(late, share)]


def multiply(spot, sizes, inverse, depth, named):
    names = tuple(n[:3] for n in named)
    pieces = [n[3] for n in named]
    rows, width = inverse.shape
    cols = pieces[0].shape[1]
    chunks = 3
    return pl.pallas_call(
        functools.partial(multiply_body, names),
        out_shape=[
            jax.ShapeDtypeStruct((rows, cols), F32),
            jax.ShapeDtypeStruct((rows, depth * PARTS), BF16),
        ],
        in_specs=[SMEM, SMEM, HBM] + [VMEM] * len(pieces),
        out_specs=[VMEM, VMEM],
        scratch_shapes=[
            pltpu.VMEM((chunks, rows // chunks, width), BF16),
            pltpu.VMEM((width, cols), BF16),
            pltpu.SemaphoreType.DMA((chunks,)),
        ],
        compiler_params=params(),
        cost_estimate=pl.CostEstimate(
            flops=2 * rows * width * cols, bytes_accessed=2 * rows * width, transcendentals=0
        ),
    )(spot, sizes, inverse, *pieces)


def contribute_body(spot_ref, sizes_ref, total_ref, later_ref, lower_ref, *refs):
    pieces, carriers, outs = refs[:PARTS], refs[PARTS:-11], refs[-11:-3]
    top_ref, right, product_ref = refs[-3:]
    live, row = sizes_ref[spot_ref[1]], spot_ref[0]
    depth = later_ref.shape[1] // PARTS
    for k, carrier in enumerate((*carriers, pieces[0])):
        top_ref[k] = carrier[depth:]
    first = source_rows(spot_ref, 3, 1) * PARTS * depth
    for part, piece in enumerate(pieces):
        place = part * depth
        right[place : place + depth] = live_rows(piece[:depth], first + place, live)
    total = total_ref[...] + jnp.dot(later_ref[...], right[...], preferred_element_type=F32)
    solved = live_rows(total, row * total.shape[0], live)
    product_ref[...] = jnp.dot(lower_ref[...], solved, preferred_element_type=F32)
    z, y = row // 2, row & 1
    slabs, height, _ = outs[0].shape
    for k in range(4):
        for j in range(slabs):
            base = j * BLOCK + (z ^ k) * 2 * height
            mine = pl.multiple_of(base + y * height, height)
            other = pl.multiple_of(base + (1 - y) * height, height)
            outs[k][j] = product_ref[pl.ds(mine, height)]
            outs[4 + k][j] = product_ref[pl.ds(other, height)].astype(BF16)


def contribute(spot, sizes, total, later, lower, pieces, carriers):
    border, rows = lower.shape
    cols = total.shape[1]
    slot = (border // BLOCK, BLOCK // 8, cols)
    count = len(carriers) + 1
    tops = (count, pieces[0].shape[0] - later.shape[1] // PARTS, cols)
    out = pl.pallas_call(
        contribute_body,
        out_shape=[jax.ShapeDtypeStruct(slot, F32)] * 4
        + [jax.ShapeDtypeStruct(slot, BF16)] * 4
        + [jax.ShapeDtypeStruct(tops, BF16)],
        in_specs=[SMEM, SMEM] + [VMEM] * (3 + len(pieces) + len(carriers)),
        out_specs=[VMEM] * 9,
        scratch_shapes=[
            pltpu.VMEM((later.shape[1], cols), BF16),
            pltpu.VMEM((border, cols), F32),
        ],
        compiler_params=params(),
        cost_estimate=pl.CostEstimate(
            flops=2 * rows * cols * (later.shape[1] + border),
            bytes_accessed=2 * rows * (later.shape[1] + border),
            transcendentals=0,
        ),
    )(spot, sizes, total, later, lower, *pieces, *carriers)
    return out[:4], out[4:8], out[8]


def place_body(targets_ref, spot_ref, *refs):
    pieces, slots_ref, total_ref = refs[:4], refs[4], refs[5]
    total_ref[...] = jnp.zeros_like(total_ref)
    blocks = total_ref.shape[0]
    slabs = pieces[0].shape[0]
    group = spot_ref[1]
    first = group * blocks
    for k, piece in enumerate(pieces):
        for j in range(slabs):
            place = targets_ref[group ^ k, j] - first

            @pl.when((place >= 0) & (place < blocks))
            def _():
                total_ref[place] += piece[j].astype(F32)

    slots_ref[...] = total_ref[...].astype(BF16)


def place(targets, spot, pieces, blocks):
    shape = (blocks,) + pieces[0].shape[1:]
    return pl.pallas_call(
        place_body,
        out_shape=jax.ShapeDtypeStruct(shape, BF16),
        in_specs=[pl.BlockSpec(memory_space=pltpu.SMEM)] * 2
        + [pl.BlockSpec(memory_space=pltpu.VMEM)] * 4,
        out_specs=pl.BlockSpec(memory_space=pltpu.VMEM),
        scratch_shapes=[pltpu.VMEM(shape, F32)],
        compiler_params=params(),
    )(targets, spot, *pieces)


ORDER = ((0, 0), (0, 1), (1, 0), (1, 1), (2, 0), (2, 1), (3, 0), (3, 1))


def reorder_body(spot_ref, order_ref, inverse_ref, *out_refs):
    row, core = spot_ref[0], spot_ref[1] & 1
    half, width = inverse_ref.shape[0] // 2, inverse_ref.shape[1]
    rows = (row * 2 + core) * half + lax.broadcasted_iota(jnp.int32, (half, width), 0)
    cols = lax.broadcasted_iota(jnp.int32, (half, width), 1)
    mine = inverse_ref[pl.ds(pl.multiple_of(core * half, half), half)].astype(F32)
    lower = jnp.where(cols < rows, mine, jnp.where(cols == rows, 1.0, 0.0)).astype(BF16)
    for side, out_ref in ((core, out_refs[0]), (1 - core, out_refs[1])):
        picks = []
        for steps, crossed in ORDER:
            first = (source_rows(spot_ref, steps, crossed) * 2 + side) * half
            ids = first + lax.broadcasted_iota(jnp.int32, (half, width), 0)
            picks.append((ids == order_ref[...]).astype(F32).astype(BF16))
        pick = jnp.concatenate(picks)
        moved = lax.dot_general(
            lower, pick, (((1,), (1,)), ((), ())), preferred_element_type=F32
        )
        out_ref[...] = moved.astype(BF16)


def reorder(spot, order, inverse):
    half, width = inverse.shape[0] // 2, inverse.shape[1]
    return pl.pallas_call(
        reorder_body,
        out_shape=[jax.ShapeDtypeStruct((half, width // 2), BF16)] * 2,
        in_specs=[SMEM, VMEM, VMEM],
        out_specs=[VMEM, VMEM],
        compiler_params=params(),
    )(spot, order[None], inverse)


def factor_body(mine_ref, other_ref, top_ref, came_ref, out_ref):
    count, half, cols = top_ref.shape
    total = jnp.dot(
        mine_ref[...], top_ref[...].reshape(count * half, cols), preferred_element_type=F32
    ) + jnp.dot(
        other_ref[...], came_ref[...].reshape(count * half, cols), preferred_element_type=F32
    )
    out_ref[...] = total.astype(BF16)


def panel_factor(mine, other, top, came):
    return pl.pallas_call(
        factor_body,
        out_shape=jax.ShapeDtypeStruct((mine.shape[0], top.shape[-1]), BF16),
        in_specs=[VMEM] * 4,
        out_specs=VMEM,
        compiler_params=params(),
    )(mine, other, top, came)


def base_body(place_ref, surface_ref, lower_ref, mine_ref, other_ref, out_ref, factor_ref):
    row, core = place_ref[0], place_ref[1] & 1
    half = mine_ref.shape[1]
    for ref, side in ((mine_ref, core), (other_ref, 1 - core)):
        for k in range(mine_ref.shape[0]):
            first = pl.multiple_of(((row ^ k) * 2 + side) * half, half)
            factor_ref[pl.ds(first, half)] = ref[k]
    product = jnp.dot(lower_ref[...], factor_ref[...], preferred_element_type=F32)
    out_ref[...] = surface_ref[...] - product


def panel_update(place_scalars, surface, lower, mine, other):
    return pl.pallas_call(
        base_body,
        out_shape=jax.ShapeDtypeStruct(surface.shape, F32),
        in_specs=[pl.BlockSpec(memory_space=pltpu.SMEM)]
        + [pl.BlockSpec(memory_space=pltpu.VMEM)] * 4,
        out_specs=pl.BlockSpec(memory_space=pltpu.VMEM),
        scratch_shapes=[pltpu.VMEM((lower.shape[1], surface.shape[1]), BF16)],
        compiler_params=params(),
    )(place_scalars, surface, lower, mine, other)


def staged(
    surface,
    panel_lower,
    top_rows,
    panel_inverse,
    panel_order,
    front_inverse,
    front_upper,
    front_lower,
    front_sizes,
    border_blocks,
):
    row_count = lax.axis_size("row")
    group = lax.axis_index("grp")
    row = lax.axis_index("row")
    core = group % 2
    inverse, upper, lower = front_inverse[0], front_upper[0], front_lower[0]
    spot = jnp.stack([row, group])
    inverse = pltpu.with_memory_space_constraint(inverse, pltpu.HBM)
    depth = upper.shape[0] // PARTS

    half = top_rows.shape[0] // 2
    top = lax.dynamic_slice_in_dim(top_rows, core * half, half, 0)
    a, b = jnp.concatenate([upper[:depth], top]), upper[depth:]

    ay, az, by, bz = across(a), cycle(a), across(b), cycle(b)
    lower_mine, lower_other = reorder(spot, panel_order, panel_inverse)
    ay, az, lower_mine = together((ay, az, lower_mine))
    ay1, az1 = across(az), cycle(az)
    by, bz = together((by, bz))
    by1, bz1 = across(bz), cycle(bz)
    ay1, az1 = together((ay1, az1))
    ay2, az2 = across(az1), cycle(az1)
    by1, bz1 = together((by1, bz1))
    by2, bz2 = across(bz1), cycle(bz1)
    ay2, az2 = together((ay2, az2))
    ay3 = across(az2)
    by2, bz2, ay = together((by2, bz2, ay))
    by3 = across(bz2)
    named = [(0, 0, 0, a), (0, 0, 1, b), (0, 1, 0, ay), (0, 1, 1, by)]
    named += [(1, 0, 0, az), (1, 0, 1, bz), (1, 1, 0, ay1), (1, 1, 1, by1)]
    named += [(2, 0, 0, az1), (2, 0, 1, bz1), (2, 1, 0, ay2), (2, 1, 1, by2)]
    named += [(3, 0, 0, az2), (3, 0, 1, bz2)]
    total, later = multiply(spot, front_sizes, inverse, depth, named)
    carriers = (a, ay, az, ay1, az1, ay2, az2)
    keep, send, top_mine = contribute(
        spot, front_sizes, total, later, lower, (ay3, by3), carriers
    )

    top_other = group_swap(top_mine, 1)
    come = {k: across(send[k]) for k in (3, 2, 1, 0)}
    sums = [keep[k] + come[k].astype(F32) for k in range(4)]
    for k in (3, 2, 1):
        sums[k] = along(sums[k].astype(BF16), k).astype(F32)
    factor = panel_factor(lower_mine, lower_other, top_mine, top_other)
    factor_y = across(factor)
    mine = (sums[0] + sums[1] + sums[2] + sums[3]).astype(BF16)
    mine, factor_y = together((mine, factor_y))
    factor2 = jnp.stack([factor, factor_y])
    factor2_in = along(factor2, 1)
    pieces = [mine] + [group_swap(mine, k) for k in (1, 2, 3)]
    local_blocks = surface.shape[0] // BLOCK
    blocks = local_blocks * row_count
    slots = place(border_blocks, spot, pieces, blocks)
    slots, factor2_in = together((slots, factor2_in))
    factor4 = jnp.concatenate([factor2, factor2_in])
    factor_mine = jnp.concatenate([factor4, along(factor4, 2)])
    factor_other = group_swap(factor_mine, 1)
    base = panel_update(spot, surface, panel_lower, factor_mine, factor_other)
    slots = slots.reshape((row_count, local_blocks) + slots.shape[1:])
    got = lax.all_to_all(slots, "row", 0, 0, tiled=True)
    collected = got.transpose(1, 0, 2, 3).reshape(surface.shape).astype(F32)
    return base - collected


def gathered(
    surface,
    panel_lower,
    top_rows,
    panel_inverse,
    panel_order,
    front_inverse,
    front_upper,
    front_lower,
    front_sizes,
    border_blocks,
):
    row_count = lax.axis_size("row")
    grp_index = lax.axis_index("grp")
    row_index = lax.axis_index("row")
    inverse_rows, upper_local, lower_local = front_inverse[0], front_upper[0], front_lower[0]
    local_piv, col_count = upper_local.shape
    pivot_ids = row_index * local_piv + jnp.arange(local_piv, dtype=jnp.int32)
    live_mask = pivot_ids < front_sizes[grp_index]
    upper_kept = jnp.where(live_mask[:, None], upper_local, jnp.zeros_like(upper_local))
    lower_kept = jnp.where(live_mask[None, :], lower_local, jnp.zeros_like(lower_local))
    upper_all = lax.all_gather(upper_kept, "row", axis=0, tiled=True)
    solved = jnp.dot(inverse_rows, upper_all, preferred_element_type=F32).astype(BF16)
    partial_sum = jnp.dot(lower_kept, solved, preferred_element_type=F32)
    own_share = lax.psum_scatter(partial_sum, "row", scatter_dimension=0, tiled=True)
    contributions = lax.all_gather(own_share, ("grp", "row"), axis=0, tiled=True)
    local_blocks = surface.shape[0] // BLOCK
    device_id = grp_index * row_count + row_index
    own_ids = device_id * local_blocks + jnp.arange(local_blocks, dtype=jnp.int32)
    targets = border_blocks.reshape(-1)
    selector = (own_ids[:, None] == targets[None, :]).astype(F32)
    slabs = contributions.reshape(targets.shape[0], BLOCK * col_count)
    collected = jnp.dot(
        selector, slabs, precision=lax.Precision.HIGHEST, preferred_element_type=F32
    ).reshape(surface.shape)
    local_panel, panel_width = panel_inverse.shape
    panel_ids = jnp.arange(panel_width, dtype=jnp.int32)
    top_all = lax.all_gather(top_rows, "row", axis=0, tiled=True)
    ordered = jnp.take(top_all, panel_order, axis=0)
    own_rows = row_index * local_panel + jnp.arange(local_panel, dtype=jnp.int32)
    strict = jnp.where(
        panel_ids[None, :] < own_rows[:, None], panel_inverse, jnp.zeros_like(panel_inverse)
    )
    own_top = lax.dynamic_slice_in_dim(ordered, row_index * local_panel, local_panel, 0)
    product = jnp.dot(strict, ordered, preferred_element_type=F32)
    own_solved = (product + own_top.astype(F32)).astype(BF16)
    factor = lax.all_gather(own_solved, "row", axis=0, tiled=True)
    return surface - collected - jnp.dot(panel_lower, factor, preferred_element_type=F32)


def solution(mesh):
    in_specs = (
        P(("grp", "row"), None),
        P(("grp", "row"), None),
        P("row", None),
        P("row", None),
        P(),
        P("grp", "row", None),
        P("grp", "row", None),
        P("grp", None, "row"),
        P(),
        P(),
    )
    out_specs = P(("grp", "row"), None)
    small = mesh.shape["row"] == 8 and mesh.shape["grp"] == 4
    return jax.shard_map(
        staged if small else gathered,
        mesh=mesh,
        in_specs=in_specs,
        out_specs=out_specs,
        check_vma=False,
    )
```

```python
import functools

import jax
import jax.numpy as jnp
from jax import lax
from jax.experimental import pallas as pl
from jax.experimental.pallas import tpu as pltpu
from jax.sharding import PartitionSpec as P

BLOCK = 128
PARTS = 2
ORDER = (0, -1, 1, -2, 2, -3, 3, 4)
LIMIT = 20 << 20
F32 = jnp.float32
BF16 = jnp.bfloat16
together = lax.optimization_barrier


def params():
    return pltpu.CompilerParams(vmem_limit_bytes=LIMIT)


def row_permute(value, target):
    pairs = [(z * 2 + y, target(z, y)) for z in range(4) for y in range(2)]
    return lax.ppermute(value, "row", [(s, t[0] * 2 + t[1]) for s, t in pairs])


def ring_place(row):
    z, y = row // 2, row & 1
    return z + y * (7 - 2 * z)


def ring_row(place):
    y = place >> 2
    return (place + y * (7 - 2 * place)) * 2 + y


def ring_send(value, step):
    pairs = [(r, ring_row((ring_place(r) + step) & 7)) for r in range(8)]
    return lax.ppermute(value, "row", pairs)


def across(value):
    return row_permute(value, lambda z, y: (z, 1 - y))


def along(value, step):
    return row_permute(value, lambda z, y: (z ^ step, y))


def group_swap(value, step):
    return lax.ppermute(value, "grp", [(g, g ^ step) for g in range(4)])


SMEM = pl.BlockSpec(memory_space=pltpu.SMEM)
VMEM = pl.BlockSpec(memory_space=pltpu.VMEM)
HBM = pl.BlockSpec(memory_space=pltpu.HBM)


def source_row(spot_ref, offset):
    return ring_row((ring_place(spot_ref[0]) + offset) & 7)


def live_rows(piece, first, live):
    ids = lax.broadcasted_iota(jnp.int32, piece.shape, 0)
    return jnp.where(ids < live - first, piece.astype(F32), 0.0).astype(BF16)


def multiply_body(parts_in, depth, has_total, late, spot_ref, sizes_ref, inverse_ref, *refs):
    refs = list(refs)
    pieces = [refs.pop(0) for _ in parts_in]
    before_ref = refs.pop(0) if has_total else None
    total_ref = refs.pop(0)
    later_ref = refs.pop(0) if late else None
    left, right, sem = refs
    share = depth * PARTS
    offsets = [offset for offset, part in parts_in if part == 0]
    copies, firsts = [], []
    for i, offset in enumerate(offsets + [4] * late):
        firsts.append(pl.multiple_of(source_row(spot_ref, offset) * share, share))
        columns = inverse_ref.at[:, pl.ds(firsts[i], share)]
        out = later_ref if i == len(offsets) else left.at[:, i * share : (i + 1) * share]
        copies.append(pltpu.make_async_copy(columns, out, sem.at[i]))
        copies[i].start()
    live = sizes_ref[spot_ref[1]]
    for (offset, part), piece in zip(parts_in, pieces):
        i = offsets.index(offset)
        start = i * share + part * depth
        rows = live_rows(piece[:depth], firsts[i] + part * depth, live)
        right[start : start + depth] = rows
    total = before_ref[...] if has_total else None
    for i in range(len(offsets)):
        copies[i].wait()
        place = slice(i * share, (i + 1) * share)
        part = jnp.dot(left[:, place], right[place], preferred_element_type=F32)
        total = part if total is None else total + part
    total_ref[...] = total
    if late:
        copies[-1].wait()


def multiply(spot, sizes, inverse, depth, named, total=None, late=False):
    parts_in = tuple(n[:2] for n in named)
    pieces = [n[2] for n in named]
    extra = [] if total is None else [total]
    rows, cols = inverse.shape[0], pieces[0].shape[1]
    share = depth * PARTS
    width = depth * len(named)
    out_shape = [jax.ShapeDtypeStruct((rows, cols), F32)]
    if late:
        out_shape.append(jax.ShapeDtypeStruct((rows, share), BF16))
    inverse = pltpu.with_memory_space_constraint(inverse, pltpu.HBM)
    return pl.pallas_call(
        functools.partial(multiply_body, parts_in, depth, bool(extra), late),
        out_shape=out_shape,
        in_specs=[SMEM, SMEM, HBM] + [VMEM] * (len(pieces) + len(extra)),
        out_specs=[VMEM] * len(out_shape),
        scratch_shapes=[
            pltpu.VMEM((rows, width), BF16),
            pltpu.VMEM((width, cols), BF16),
            pltpu.SemaphoreType.DMA((width // share + late,)),
        ],
        compiler_params=params(),
        cost_estimate=pl.CostEstimate(
            flops=2 * rows * width * cols, bytes_accessed=2 * rows * width, transcendentals=0
        ),
    )(spot, sizes, inverse, *pieces, *extra)


def contribute_body(spot_ref, sizes_ref, total_ref, later_ref, lower_ref, *refs):
    pieces, carriers, outs = refs[:PARTS], refs[PARTS:-11], refs[-11:-3]
    top_ref, right, product_ref = refs[-3:]
    live, row = sizes_ref[spot_ref[1]], spot_ref[0]
    depth = later_ref.shape[1] // PARTS
    for k, carrier in enumerate((*carriers, pieces[0])):
        top_ref[k] = carrier[depth:]
    first = source_row(spot_ref, 4) * PARTS * depth
    for part, piece in enumerate(pieces):
        place = part * depth
        right[place : place + depth] = live_rows(piece[:depth], first + place, live)
    total = total_ref[...] + jnp.dot(later_ref[...], right[...], preferred_element_type=F32)
    solved = live_rows(total, row * total.shape[0], live)
    product_ref[...] = jnp.dot(lower_ref[...], solved, preferred_element_type=F32)
    z, y = row // 2, row & 1
    slabs, height, _ = outs[0].shape
    for k in range(4):
        for j in range(slabs):
            base = j * BLOCK + (z ^ k) * 2 * height
            mine = pl.multiple_of(base + y * height, height)
            other = pl.multiple_of(base + (1 - y) * height, height)
            outs[k][j] = product_ref[pl.ds(mine, height)]
            outs[4 + k][j] = product_ref[pl.ds(other, height)].astype(BF16)


def contribute(spot, sizes, total, later, lower, pieces, carriers):
    border, rows = lower.shape
    cols = total.shape[1]
    slot = (border // BLOCK, BLOCK // 8, cols)
    count = len(carriers) + 1
    tops = (count, pieces[0].shape[0] - later.shape[1] // PARTS, cols)
    out = pl.pallas_call(
        contribute_body,
        out_shape=[jax.ShapeDtypeStruct(slot, F32)] * 4
        + [jax.ShapeDtypeStruct(slot, BF16)] * 4
        + [jax.ShapeDtypeStruct(tops, BF16)],
        in_specs=[SMEM, SMEM] + [VMEM] * (3 + len(pieces) + len(carriers)),
        out_specs=[VMEM] * 9,
        scratch_shapes=[
            pltpu.VMEM((later.shape[1], cols), BF16),
            pltpu.VMEM((border, cols), F32),
        ],
        compiler_params=params(),
        cost_estimate=pl.CostEstimate(
            flops=2 * rows * cols * (later.shape[1] + border),
            bytes_accessed=2 * rows * (later.shape[1] + border),
            transcendentals=0,
        ),
    )(spot, sizes, total, later, lower, *pieces, *carriers)
    return out[:4], out[4:8], out[8]


def place_body(targets_ref, spot_ref, *refs):
    pieces, slots_ref, total_ref = refs[:4], refs[4], refs[5]
    total_ref[...] = jnp.zeros_like(total_ref)
    blocks = slots_ref.shape[0]
    slabs = pieces[0].shape[0]
    group = spot_ref[1]
    first = group * blocks
    for k, piece in enumerate(pieces):
        for j in range(slabs):
            place = targets_ref[group ^ k, j] - first

            place = jnp.where((place >= 0) & (place < blocks), place, blocks)
            total_ref[place] += piece[j].astype(F32)

    slots_ref[...] = total_ref[:blocks].astype(BF16)


def place(targets, spot, pieces, blocks):
    shape = (blocks,) + pieces[0].shape[1:]
    return pl.pallas_call(
        place_body,
        out_shape=jax.ShapeDtypeStruct(shape, BF16),
        in_specs=[pl.BlockSpec(memory_space=pltpu.SMEM)] * 2
        + [pl.BlockSpec(memory_space=pltpu.VMEM)] * 4,
        out_specs=pl.BlockSpec(memory_space=pltpu.VMEM),
        scratch_shapes=[pltpu.VMEM((blocks + 1,) + shape[1:], F32)],
        compiler_params=params(),
    )(targets, spot, *pieces)


def reorder_body(spot_ref, order_ref, inverse_ref, *out_refs):
    row, core = spot_ref[0], spot_ref[1] & 1
    half, width = inverse_ref.shape[0] // 2, inverse_ref.shape[1]
    rows = (row * 2 + core) * half + lax.broadcasted_iota(jnp.int32, (half, width), 0)
    cols = lax.broadcasted_iota(jnp.int32, (half, width), 1)
    mine = inverse_ref[pl.ds(pl.multiple_of(core * half, half), half)].astype(F32)
    lower = jnp.where(cols < rows, mine, jnp.where(cols == rows, 1.0, 0.0)).astype(BF16)
    for side, out_ref in ((core, out_refs[0]), (1 - core, out_refs[1])):
        picks = []
        for offset in ORDER:
            first = (source_row(spot_ref, offset) * 2 + side) * half
            ids = first + lax.broadcasted_iota(jnp.int32, (half, width), 0)
            picks.append((ids == order_ref[...]).astype(F32).astype(BF16))
        pick = jnp.concatenate(picks)
        moved = lax.dot_general(
            lower, pick, (((1,), (1,)), ((), ())), preferred_element_type=F32
        )
        out_ref[...] = moved.astype(BF16)


def reorder(spot, order, inverse):
    half, width = inverse.shape[0] // 2, inverse.shape[1]
    return pl.pallas_call(
        reorder_body,
        out_shape=[jax.ShapeDtypeStruct((half, width // 2), BF16)] * 2,
        in_specs=[SMEM, VMEM, VMEM],
        out_specs=[VMEM, VMEM],
        compiler_params=params(),
    )(spot, order[None], inverse)


def factor_body(mine_ref, other_ref, top_ref, came_ref, out_ref):
    count, half, cols = top_ref.shape
    total = jnp.dot(
        mine_ref[...], top_ref[...].reshape(count * half, cols), preferred_element_type=F32
    ) + jnp.dot(
        other_ref[...], came_ref[...].reshape(count * half, cols), preferred_element_type=F32
    )
    out_ref[...] = total.astype(BF16)


def panel_factor(mine, other, top, came):
    return pl.pallas_call(
        factor_body,
        out_shape=jax.ShapeDtypeStruct((mine.shape[0], top.shape[-1]), BF16),
        in_specs=[VMEM] * 4,
        out_specs=VMEM,
        compiler_params=params(),
    )(mine, other, top, came)


def base_body(place_ref, surface_ref, lower_ref, mine_ref, other_ref, out_ref, factor_ref):
    row, core = place_ref[0], place_ref[1] & 1
    half = mine_ref.shape[1]
    for ref, side in ((mine_ref, core), (other_ref, 1 - core)):
        for k, apart in enumerate((0, 1, 4, 5, 2, 3, 6, 7)):
            first = pl.multiple_of(((row ^ apart) * 2 + side) * half, half)
            factor_ref[pl.ds(first, half)] = ref[k]
    product = jnp.dot(lower_ref[...], factor_ref[...], preferred_element_type=F32)
    out_ref[...] = surface_ref[...] - product


def panel_update(place_scalars, surface, lower, mine, other):
    return pl.pallas_call(
        base_body,
        out_shape=jax.ShapeDtypeStruct(surface.shape, F32),
        in_specs=[pl.BlockSpec(memory_space=pltpu.SMEM)]
        + [pl.BlockSpec(memory_space=pltpu.VMEM)] * 4,
        out_specs=pl.BlockSpec(memory_space=pltpu.VMEM),
        scratch_shapes=[pltpu.VMEM((lower.shape[1], surface.shape[1]), BF16)],
        compiler_params=params(),
    )(place_scalars, surface, lower, mine, other)


def staged(
    surface,
    panel_lower,
    top_rows,
    panel_inverse,
    panel_order,
    front_inverse,
    front_upper,
    front_lower,
    front_sizes,
    border_blocks,
):
    row_count = lax.axis_size("row")
    group = lax.axis_index("grp")
    row = lax.axis_index("row")
    core = group % 2
    inverse, upper, lower = front_inverse[0], front_upper[0], front_lower[0]
    spot = jnp.stack([row, group])
    inverse = pltpu.with_memory_space_constraint(inverse, pltpu.HBM)
    depth = upper.shape[0] // PARTS

    half = top_rows.shape[0] // 2
    top = lax.dynamic_slice_in_dim(top_rows, core * half, half, 0)
    a, b = jnp.concatenate([upper[:depth], top]), upper[depth:]

    fold = functools.partial(multiply, spot, front_sizes, inverse, depth)
    a_up, a_down, b_up, b_down = ring_send(a, 1), ring_send(a, -1), ring_send(b, 1), ring_send(b, -1)
    lower_mine, lower_other = reorder(spot, panel_order, panel_inverse)
    a_up, a_down, lower_mine = together((a_up, a_down, lower_mine))
    a_up2, a_down2 = ring_send(a_up, 1), ring_send(a_down, -1)
    b_up, b_down = together((b_up, b_down))
    b_up2, b_down2 = ring_send(b_up, 1), ring_send(b_down, -1)
    named = [(0, 0, a), (0, 1, b), (-1, 0, a_up), (-1, 1, b_up), (1, 0, a_down), (1, 1, b_down)]
    (total,) = fold(named)
    a_up2, a_down2, total = together((a_up2, a_down2, total))
    a_up3, a_down3 = ring_send(a_up2, 1), ring_send(a_down2, -1)
    b_up2, b_down2 = together((b_up2, b_down2))
    b_up3, b_down3 = ring_send(b_up2, 1), ring_send(b_down2, -1)
    named = [(-2, 0, a_up2), (-2, 1, b_up2), (2, 0, a_down2), (2, 1, b_down2)]
    (total,) = fold(named, total)
    a_up3, a_down3, total = together((a_up3, a_down3, total))
    a4 = ring_send(a_up3, 1)
    b_up3, b_down3 = together((b_up3, b_down3))
    b4 = ring_send(b_down3, -1)
    named = [(-3, 0, a_up3), (-3, 1, b_up3), (3, 0, a_down3), (3, 1, b_down3)]
    total, later = fold(named, total, late=True)
    carriers = (a, a_up, a_down, a_up2, a_down2, a_up3, a_down3)
    keep, send, top_mine = contribute(
        spot, front_sizes, total, later, lower, (a4, b4), carriers
    )

    top_other = group_swap(top_mine, 1)
    come = {k: across(send[k]) for k in (3, 2, 1, 0)}
    sums = [keep[k] + come[k].astype(F32) for k in range(4)]
    for k in (3, 2, 1):
        sums[k] = along(sums[k].astype(BF16), k).astype(F32)
    factor = panel_factor(lower_mine, lower_other, top_mine, top_other)
    factor_y = across(factor)
    mine = (sums[0] + sums[1] + sums[2] + sums[3]).astype(BF16)
    mine, factor_y = together((mine, factor_y))
    factor2 = jnp.stack([factor, factor_y])
    factor2_in = along(factor2, 2)
    pieces = [mine] + [group_swap(mine, k) for k in (1, 2, 3)]
    local_blocks = surface.shape[0] // BLOCK
    blocks = local_blocks * row_count
    slots = place(border_blocks, spot, pieces, blocks)
    slots, factor2_in = together((slots, factor2_in))
    factor4 = jnp.concatenate([factor2, factor2_in])
    factor_mine = jnp.concatenate([factor4, along(factor4, 1)])
    factor_other = group_swap(factor_mine, 1)
    base = panel_update(spot, surface, panel_lower, factor_mine, factor_other)
    slots = slots.reshape((row_count, local_blocks) + slots.shape[1:])
    got = lax.all_to_all(slots, "row", 0, 0, tiled=True)
    collected = got.transpose(1, 0, 2, 3).reshape(surface.shape).astype(F32)
    return base - collected


def gathered(
    surface,
    panel_lower,
    top_rows,
    panel_inverse,
    panel_order,
    front_inverse,
    front_upper,
    front_lower,
    front_sizes,
    border_blocks,
):
    row_count = lax.axis_size("row")
    grp_index = lax.axis_index("grp")
    row_index = lax.axis_index("row")
    inverse_rows, upper_local, lower_local = front_inverse[0], front_upper[0], front_lower[0]
    local_piv, col_count = upper_local.shape
    pivot_ids = row_index * local_piv + jnp.arange(local_piv, dtype=jnp.int32)
    live_mask = pivot_ids < front_sizes[grp_index]
    upper_kept = jnp.where(live_mask[:, None], upper_local, jnp.zeros_like(upper_local))
    lower_kept = jnp.where(live_mask[None, :], lower_local, jnp.zeros_like(lower_local))
    upper_all = lax.all_gather(upper_kept, "row", axis=0, tiled=True)
    solved = jnp.dot(inverse_rows, upper_all, preferred_element_type=F32).astype(BF16)
    partial_sum = jnp.dot(lower_kept, solved, preferred_element_type=F32)
    own_share = lax.psum_scatter(partial_sum, "row", scatter_dimension=0, tiled=True)
    contributions = lax.all_gather(own_share, ("grp", "row"), axis=0, tiled=True)
    local_blocks = surface.shape[0] // BLOCK
    device_id = grp_index * row_count + row_index
    own_ids = device_id * local_blocks + jnp.arange(local_blocks, dtype=jnp.int32)
    targets = border_blocks.reshape(-1)
    selector = (own_ids[:, None] == targets[None, :]).astype(F32)
    slabs = contributions.reshape(targets.shape[0], BLOCK * col_count)
    collected = jnp.dot(
        selector, slabs, precision=lax.Precision.HIGHEST, preferred_element_type=F32
    ).reshape(surface.shape)
    local_panel, panel_width = panel_inverse.shape
    panel_ids = jnp.arange(panel_width, dtype=jnp.int32)
    top_all = lax.all_gather(top_rows, "row", axis=0, tiled=True)
    ordered = jnp.take(top_all, panel_order, axis=0)
    own_rows = row_index * local_panel + jnp.arange(local_panel, dtype=jnp.int32)
    strict = jnp.where(
        panel_ids[None, :] < own_rows[:, None], panel_inverse, jnp.zeros_like(panel_inverse)
    )
    own_top = lax.dynamic_slice_in_dim(ordered, row_index * local_panel, local_panel, 0)
    product = jnp.dot(strict, ordered, preferred_element_type=F32)
    own_solved = (product + own_top.astype(F32)).astype(BF16)
    factor = lax.all_gather(own_solved, "row", axis=0, tiled=True)
    return surface - collected - jnp.dot(panel_lower, factor, preferred_element_type=F32)


def solution(mesh):
    in_specs = (
        P(("grp", "row"), None),
        P(("grp", "row"), None),
        P("row", None),
        P("row", None),
        P(),
        P("grp", "row", None),
        P("grp", "row", None),
        P("grp", None, "row"),
        P(),
        P(),
    )
    out_specs = P(("grp", "row"), None)
    small = mesh.shape["row"] == 8 and mesh.shape["grp"] == 4
    return jax.shard_map(
        staged if small else gathered,
        mesh=mesh,
        in_specs=in_specs,
        out_specs=out_specs,
        check_vma=False,
    )
```

```python
import functools

import jax
import jax.numpy as jnp
from jax import lax
from jax.experimental import pallas as pl
from jax.experimental.pallas import tpu as pltpu
from jax.sharding import PartitionSpec as P

BLOCK = 128
PARTS = 2
ORDER = (0, -1, 1, -2, 2, -3, 3, 4)
LIMIT = 20 << 20
F32 = jnp.float32
BF16 = jnp.bfloat16
together = lax.optimization_barrier


def params():
    return pltpu.CompilerParams(vmem_limit_bytes=LIMIT)


def row_permute(value, target):
    pairs = [(z * 2 + y, target(z, y)) for z in range(4) for y in range(2)]
    return lax.ppermute(value, "row", [(s, t[0] * 2 + t[1]) for s, t in pairs])


def ring_place(row):
    z, y = row // 2, row & 1
    return z + y * (7 - 2 * z)


def ring_row(place):
    y = place >> 2
    return (place + y * (7 - 2 * place)) * 2 + y


def ring_send(value, step):
    pairs = [(r, ring_row((ring_place(r) + step) & 7)) for r in range(8)]
    return lax.ppermute(value, "row", pairs)


def across(value):
    return row_permute(value, lambda z, y: (z, 1 - y))


def along(value, step):
    return row_permute(value, lambda z, y: (z ^ step, y))


def group_swap(value, step):
    return lax.ppermute(value, "grp", [(g, g ^ step) for g in range(4)])


SMEM = pl.BlockSpec(memory_space=pltpu.SMEM)
VMEM = pl.BlockSpec(memory_space=pltpu.VMEM)
HBM = pl.BlockSpec(memory_space=pltpu.HBM)


def source_row(spot_ref, offset):
    return ring_row((ring_place(spot_ref[0]) + offset) & 7)


def live_rows(piece, first, live):
    ids = lax.broadcasted_iota(jnp.int32, piece.shape, 0)
    return jnp.where(ids < live - first, piece.astype(F32), 0.0).astype(BF16)


def multiply_body(parts_in, depth, has_total, late, spot_ref, sizes_ref, inverse_ref, *refs):
    refs = list(refs)
    pieces = [refs.pop(0) for _ in parts_in]
    before_ref = refs.pop(0) if has_total else None
    total_ref = refs.pop(0)
    later_ref = refs.pop(0) if late else None
    left, right, sem = refs
    share = depth * PARTS
    offsets = [offset for offset, part in parts_in if part == 0]
    copies, firsts = [], []
    for i, offset in enumerate(offsets + [4] * late):
        firsts.append(pl.multiple_of(source_row(spot_ref, offset) * share, share))
        columns = inverse_ref.at[:, pl.ds(firsts[i], share)]
        out = later_ref if i == len(offsets) else left.at[:, i * share : (i + 1) * share]
        copies.append(pltpu.make_async_copy(columns, out, sem.at[i]))
        copies[i].start()
    live = sizes_ref[spot_ref[1]]
    for (offset, part), piece in zip(parts_in, pieces):
        i = offsets.index(offset)
        start = i * share + part * depth
        rows = live_rows(piece[:depth], firsts[i] + part * depth, live)
        right[start : start + depth] = rows
    total = before_ref[...] if has_total else None
    for i in range(len(offsets)):
        copies[i].wait()
        place = slice(i * share, (i + 1) * share)
        part = jnp.dot(left[:, place], right[place], preferred_element_type=F32)
        total = part if total is None else total + part
    total_ref[...] = total
    if late:
        copies[-1].wait()


def multiply(spot, sizes, inverse, depth, named, total=None, late=False):
    parts_in = tuple(n[:2] for n in named)
    pieces = [n[2] for n in named]
    extra = [] if total is None else [total]
    rows, cols = inverse.shape[0], pieces[0].shape[1]
    share = depth * PARTS
    width = depth * len(named)
    out_shape = [jax.ShapeDtypeStruct((rows, cols), F32)]
    if late:
        out_shape.append(jax.ShapeDtypeStruct((rows, share), BF16))
    inverse = pltpu.with_memory_space_constraint(inverse, pltpu.HBM)
    return pl.pallas_call(
        functools.partial(multiply_body, parts_in, depth, bool(extra), late),
        out_shape=out_shape,
        in_specs=[SMEM, SMEM, HBM] + [VMEM] * (len(pieces) + len(extra)),
        out_specs=[VMEM] * len(out_shape),
        scratch_shapes=[
            pltpu.VMEM((rows, width), BF16),
            pltpu.VMEM((width, cols), BF16),
            pltpu.SemaphoreType.DMA((width // share + late,)),
        ],
        compiler_params=params(),
        cost_estimate=pl.CostEstimate(
            flops=2 * rows * width * cols, bytes_accessed=2 * rows * width, transcendentals=0
        ),
    )(spot, sizes, inverse, *pieces, *extra)


def contribute_body(spot_ref, sizes_ref, total_ref, later_ref, lower_ref, *refs):
    pieces, carriers, outs = refs[:PARTS], refs[PARTS:-10], refs[-10:-3]
    top_ref, right, product_ref = refs[-3:]
    live, row = sizes_ref[spot_ref[1]], spot_ref[0]
    depth = later_ref.shape[1] // PARTS
    for k, carrier in enumerate((*carriers, pieces[0])):
        top_ref[k] = carrier[depth:]
    first = source_row(spot_ref, 4) * PARTS * depth
    for part, piece in enumerate(pieces):
        place = part * depth
        right[place : place + depth] = live_rows(piece[:depth], first + place, live)
    total = total_ref[...] + jnp.dot(later_ref[...], right[...], preferred_element_type=F32)
    solved = live_rows(total, row * total.shape[0], live)
    product_ref[...] = jnp.dot(lower_ref[...], solved, preferred_element_type=F32)
    z, y = row // 2, row & 1
    slabs, height, _ = outs[0].shape
    for k in range(4):
        for j in range(slabs):
            base = j * BLOCK + (z ^ k) * 2 * height
            mine = pl.multiple_of(base + y * height, height)
            other = pl.multiple_of(base + (1 - y) * height, height)
            outs[k][j] = product_ref[pl.ds(mine, height)]
            sent = product_ref[pl.ds(other, height)].astype(BF16)
            if k > 1:
                outs[3 + k][j] = sent
            else:
                outs[4][k * slabs + j] = sent


def contribute(spot, sizes, total, later, lower, pieces, carriers):
    border, rows = lower.shape
    cols = total.shape[1]
    slot = (border // BLOCK, BLOCK // 8, cols)
    count = len(carriers) + 1
    tops = (count, pieces[0].shape[0] - later.shape[1] // PARTS, cols)
    out = pl.pallas_call(
        contribute_body,
        out_shape=[jax.ShapeDtypeStruct(slot, F32)] * 4
        + [jax.ShapeDtypeStruct((2 * slot[0],) + slot[1:], BF16)]
        + [jax.ShapeDtypeStruct(slot, BF16)] * 2
        + [jax.ShapeDtypeStruct(tops, BF16)],
        in_specs=[SMEM, SMEM] + [VMEM] * (3 + len(pieces) + len(carriers)),
        out_specs=[VMEM] * 8,
        scratch_shapes=[
            pltpu.VMEM((later.shape[1], cols), BF16),
            pltpu.VMEM((border, cols), F32),
        ],
        compiler_params=params(),
        cost_estimate=pl.CostEstimate(
            flops=2 * rows * cols * (later.shape[1] + border),
            bytes_accessed=2 * rows * (later.shape[1] + border),
            transcendentals=0,
        ),
    )(spot, sizes, total, later, lower, *pieces, *carriers)
    return out[:4], out[4:7], out[7]


def place_body(targets_ref, spot_ref, *refs):
    pieces, slots_ref, total_ref = refs[:4], refs[4], refs[5]
    total_ref[...] = jnp.zeros_like(total_ref)
    blocks = slots_ref.shape[0]
    slabs = pieces[0].shape[0]
    group = spot_ref[1]
    first = group * blocks
    for k, piece in enumerate(pieces):
        for j in range(slabs):
            place = targets_ref[group ^ k, j] - first

            place = jnp.where((place >= 0) & (place < blocks), place, blocks)
            total_ref[place] += piece[j].astype(F32)

    slots_ref[...] = total_ref[:blocks].astype(BF16)


def place(targets, spot, pieces, blocks):
    shape = (blocks,) + pieces[0].shape[1:]
    return pl.pallas_call(
        place_body,
        out_shape=jax.ShapeDtypeStruct(shape, BF16),
        in_specs=[pl.BlockSpec(memory_space=pltpu.SMEM)] * 2
        + [pl.BlockSpec(memory_space=pltpu.VMEM)] * 4,
        out_specs=pl.BlockSpec(memory_space=pltpu.VMEM),
        scratch_shapes=[pltpu.VMEM((blocks + 1,) + shape[1:], F32)],
        compiler_params=params(),
    )(targets, spot, *pieces)


def reorder_body(spot_ref, order_ref, inverse_ref, *out_refs):
    row, core = spot_ref[0], spot_ref[1] & 1
    half, width = inverse_ref.shape[0] // 2, inverse_ref.shape[1]
    rows = (row * 2 + core) * half + lax.broadcasted_iota(jnp.int32, (half, width), 0)
    cols = lax.broadcasted_iota(jnp.int32, (half, width), 1)
    mine = inverse_ref[pl.ds(pl.multiple_of(core * half, half), half)].astype(F32)
    lower = jnp.where(cols < rows, mine, jnp.where(cols == rows, 1.0, 0.0)).astype(BF16)
    for side, out_ref in ((core, out_refs[0]), (1 - core, out_refs[1])):
        picks = []
        for offset in ORDER:
            first = (source_row(spot_ref, offset) * 2 + side) * half
            ids = first + lax.broadcasted_iota(jnp.int32, (half, width), 0)
            picks.append((ids == order_ref[...]).astype(F32).astype(BF16))
        pick = jnp.concatenate(picks)
        moved = lax.dot_general(
            lower, pick, (((1,), (1,)), ((), ())), preferred_element_type=F32
        )
        out_ref[...] = moved.astype(BF16)


def reorder(spot, order, inverse):
    half, width = inverse.shape[0] // 2, inverse.shape[1]
    return pl.pallas_call(
        reorder_body,
        out_shape=[jax.ShapeDtypeStruct((half, width // 2), BF16)] * 2,
        in_specs=[SMEM, VMEM, VMEM],
        out_specs=[VMEM, VMEM],
        compiler_params=params(),
    )(spot, order[None], inverse)


def factor_body(mine_ref, other_ref, top_ref, came_ref, slots_ref, out_ref):
    count, half, cols = top_ref.shape
    slots = slots_ref.shape[0]
    total = jnp.dot(
        mine_ref[...], top_ref[...].reshape(count * half, cols), preferred_element_type=F32
    ) + jnp.dot(
        other_ref[...], came_ref[...].reshape(count * half, cols), preferred_element_type=F32
    )
    out_ref[:slots] = slots_ref[...]
    out_ref[slots:] = total.astype(BF16).reshape(out_ref.shape[0] - slots, -1, cols)


def panel_factor(mine, other, top, came, slots):
    count, height, cols = slots.shape
    return pl.pallas_call(
        factor_body,
        out_shape=jax.ShapeDtypeStruct((count + mine.shape[0] // height, height, cols), BF16),
        in_specs=[VMEM] * 5,
        out_specs=VMEM,
        compiler_params=params(),
    )(mine, other, top, came, slots)


def base_body(place_ref, surface_ref, lower_ref, mine_ref, other_ref, out_ref, factor_ref):
    row, core = place_ref[0], place_ref[1] & 1
    half = mine_ref.shape[1]
    for ref, side in ((mine_ref, core), (other_ref, 1 - core)):
        for k, apart in enumerate((0, 1, 4, 5, 2, 3, 6, 7)):
            first = pl.multiple_of(((row ^ apart) * 2 + side) * half, half)
            factor_ref[pl.ds(first, half)] = ref[k]
    product = jnp.dot(lower_ref[...], factor_ref[...], preferred_element_type=F32)
    out_ref[...] = surface_ref[...] - product


def panel_update(place_scalars, surface, lower, mine, other):
    return pl.pallas_call(
        base_body,
        out_shape=jax.ShapeDtypeStruct(surface.shape, F32),
        in_specs=[pl.BlockSpec(memory_space=pltpu.SMEM)]
        + [pl.BlockSpec(memory_space=pltpu.VMEM)] * 4,
        out_specs=pl.BlockSpec(memory_space=pltpu.VMEM),
        scratch_shapes=[pltpu.VMEM((lower.shape[1], surface.shape[1]), BF16)],
        compiler_params=params(),
    )(place_scalars, surface, lower, mine, other)


def staged(
    surface,
    panel_lower,
    top_rows,
    panel_inverse,
    panel_order,
    front_inverse,
    front_upper,
    front_lower,
    front_sizes,
    border_blocks,
):
    row_count = lax.axis_size("row")
    group = lax.axis_index("grp")
    row = lax.axis_index("row")
    core = group % 2
    inverse, upper, lower = front_inverse[0], front_upper[0], front_lower[0]
    spot = jnp.stack([row, group])
    inverse = pltpu.with_memory_space_constraint(inverse, pltpu.HBM)
    depth = upper.shape[0] // PARTS

    half = top_rows.shape[0] // 2
    top = lax.dynamic_slice_in_dim(top_rows, core * half, half, 0)
    a, b = jnp.concatenate([upper[:depth], top]), upper[depth:]

    fold = functools.partial(multiply, spot, front_sizes, inverse, depth)
    a_up, a_down, b_up, b_down = ring_send(a, 1), ring_send(a, -1), ring_send(b, 1), ring_send(b, -1)
    lower_mine, lower_other = reorder(spot, panel_order, panel_inverse)
    a_up, a_down, lower_mine = together((a_up, a_down, lower_mine))
    a_up2, a_down2 = ring_send(a_up, 1), ring_send(a_down, -1)
    b_up, b_down = together((b_up, b_down))
    b_up2, b_down2 = ring_send(b_up, 1), ring_send(b_down, -1)
    named = [(0, 0, a), (0, 1, b), (-1, 0, a_up), (-1, 1, b_up), (1, 0, a_down), (1, 1, b_down)]
    (total,) = fold(named)
    a_up2, a_down2, total = together((a_up2, a_down2, total))
    a_up3, a_down3 = ring_send(a_up2, 1), ring_send(a_down2, -1)
    b_up2, b_down2 = together((b_up2, b_down2))
    b_up3, b_down3 = ring_send(b_up2, 1), ring_send(b_down2, -1)
    named = [(-2, 0, a_up2), (-2, 1, b_up2), (2, 0, a_down2), (2, 1, b_down2)]
    (total,) = fold(named, total)
    a_up3, a_down3, total = together((a_up3, a_down3, total))
    a4 = ring_send(a_up3, 1)
    b_up3, b_down3 = together((b_up3, b_down3))
    b4 = ring_send(b_down3, -1)
    named = [(-3, 0, a_up3), (-3, 1, b_up3), (3, 0, a_down3), (3, 1, b_down3)]
    total, later = fold(named, total, late=True)
    carriers = (a, a_up, a_down, a_up2, a_down2, a_up3, a_down3)
    keep, send, top_mine = contribute(
        spot, front_sizes, total, later, lower, (a4, b4), carriers
    )

    top_other = group_swap(top_mine, 1)
    come3, come2 = across(send[2]), across(send[1])
    last = panel_factor(lower_mine, lower_other, top_mine, top_other, send[0])
    come10 = across(last)
    come3, come2, last = together((come3, come2, last))
    slabs = keep[0].shape[0]
    come = [come10[:slabs], come10[slabs : 2 * slabs], come2, come3]
    sums = [keep[k] + come[k].astype(F32) for k in range(4)]
    swapped = {k: along(sums[k].astype(BF16), k) for k in (3, 2, 1)}
    factor = jnp.stack([last[2 * slabs :], come10[2 * slabs :]])
    swapped[2], factor = together((swapped[2], factor))
    factor_in = along(factor, 2)
    mine = sums[0] + swapped[1].astype(F32) + swapped[2].astype(F32) + swapped[3].astype(F32)
    mine = mine.astype(BF16)
    pieces = [mine] + [group_swap(mine, k) for k in (1, 2, 3)]
    pieces[1], factor_in = together((pieces[1], factor_in))
    factor4 = jnp.concatenate([factor, factor_in])
    factor_mine = jnp.concatenate([factor4, along(factor4, 1)])
    factor_mine = factor_mine.reshape((row_count, half) + top.shape[1:])
    factor_other = group_swap(factor_mine, 1)
    base = panel_update(spot, surface, panel_lower, factor_mine, factor_other)
    local_blocks = surface.shape[0] // BLOCK
    blocks = local_blocks * row_count
    slots = place(border_blocks, spot, pieces, blocks)
    slots = slots.reshape((row_count, local_blocks) + slots.shape[1:])
    got = lax.all_to_all(slots, "row", 0, 0, tiled=True)
    collected = got.transpose(1, 0, 2, 3).reshape(surface.shape).astype(F32)
    return base - collected


def gathered(
    surface,
    panel_lower,
    top_rows,
    panel_inverse,
    panel_order,
    front_inverse,
    front_upper,
    front_lower,
    front_sizes,
    border_blocks,
):
    row_count = lax.axis_size("row")
    grp_index = lax.axis_index("grp")
    row_index = lax.axis_index("row")
    inverse_rows, upper_local, lower_local = front_inverse[0], front_upper[0], front_lower[0]
    local_piv, col_count = upper_local.shape
    pivot_ids = row_index * local_piv + jnp.arange(local_piv, dtype=jnp.int32)
    live_mask = pivot_ids < front_sizes[grp_index]
    upper_kept = jnp.where(live_mask[:, None], upper_local, jnp.zeros_like(upper_local))
    lower_kept = jnp.where(live_mask[None, :], lower_local, jnp.zeros_like(lower_local))
    upper_all = lax.all_gather(upper_kept, "row", axis=0, tiled=True)
    solved = jnp.dot(inverse_rows, upper_all, preferred_element_type=F32).astype(BF16)
    partial_sum = jnp.dot(lower_kept, solved, preferred_element_type=F32)
    own_share = lax.psum_scatter(partial_sum, "row", scatter_dimension=0, tiled=True)
    contributions = lax.all_gather(own_share, ("grp", "row"), axis=0, tiled=True)
    local_blocks = surface.shape[0] // BLOCK
    device_id = grp_index * row_count + row_index
    own_ids = device_id * local_blocks + jnp.arange(local_blocks, dtype=jnp.int32)
    targets = border_blocks.reshape(-1)
    selector = (own_ids[:, None] == targets[None, :]).astype(F32)
    slabs = contributions.reshape(targets.shape[0], BLOCK * col_count)
    collected = jnp.dot(
        selector, slabs, precision=lax.Precision.HIGHEST, preferred_element_type=F32
    ).reshape(surface.shape)
    local_panel, panel_width = panel_inverse.shape
    panel_ids = jnp.arange(panel_width, dtype=jnp.int32)
    top_all = lax.all_gather(top_rows, "row", axis=0, tiled=True)
    ordered = jnp.take(top_all, panel_order, axis=0)
    own_rows = row_index * local_panel + jnp.arange(local_panel, dtype=jnp.int32)
    strict = jnp.where(
        panel_ids[None, :] < own_rows[:, None], panel_inverse, jnp.zeros_like(panel_inverse)
    )
    own_top = lax.dynamic_slice_in_dim(ordered, row_index * local_panel, local_panel, 0)
    product = jnp.dot(strict, ordered, preferred_element_type=F32)
    own_solved = (product + own_top.astype(F32)).astype(BF16)
    factor = lax.all_gather(own_solved, "row", axis=0, tiled=True)
    return surface - collected - jnp.dot(panel_lower, factor, preferred_element_type=F32)


def solution(mesh):
    in_specs = (
        P(("grp", "row"), None),
        P(("grp", "row"), None),
        P("row", None),
        P("row", None),
        P(),
        P("grp", "row", None),
        P("grp", "row", None),
        P("grp", None, "row"),
        P(),
        P(),
    )
    out_specs = P(("grp", "row"), None)
    small = mesh.shape["row"] == 8 and mesh.shape["grp"] == 4
    return jax.shard_map(
        staged if small else gathered,
        mesh=mesh,
        in_specs=in_specs,
        out_specs=out_specs,
        check_vma=False,
    )
```

```python
import functools

import jax
import jax.numpy as jnp
from jax import lax
from jax.experimental import pallas as pl
from jax.experimental.pallas import tpu as pltpu
from jax.sharding import PartitionSpec as P

BLOCK = 128
PARTS = 2
ORDER = (0, -1, 1, -2, 2, -3, 3, 4)
LIMIT = 20 << 20
F32 = jnp.float32
BF16 = jnp.bfloat16
together = lax.optimization_barrier


def params():
    return pltpu.CompilerParams(vmem_limit_bytes=LIMIT)


def row_permute(value, target):
    pairs = [(z * 2 + y, target(z, y)) for z in range(4) for y in range(2)]
    return lax.ppermute(value, "row", [(s, t[0] * 2 + t[1]) for s, t in pairs])


def ring_place(row):
    z, y = row // 2, row & 1
    return z + y * (7 - 2 * z)


def ring_row(place):
    y = place >> 2
    return (place + y * (7 - 2 * place)) * 2 + y


def ring_send(value, step):
    pairs = [(r, ring_row((ring_place(r) + step) & 7)) for r in range(8)]
    return lax.ppermute(value, "row", pairs)


def across(value):
    return row_permute(value, lambda z, y: (z, 1 - y))


def along(value, step):
    return row_permute(value, lambda z, y: (z ^ step, y))


def group_swap(value, step):
    return lax.ppermute(value, "grp", [(g, g ^ step) for g in range(4)])


SMEM = pl.BlockSpec(memory_space=pltpu.SMEM)
VMEM = pl.BlockSpec(memory_space=pltpu.VMEM)
HBM = pl.BlockSpec(memory_space=pltpu.HBM)


def source_row(spot_ref, offset):
    return ring_row((ring_place(spot_ref[0]) + offset) & 7)


def live_rows(piece, first, live):
    ids = lax.broadcasted_iota(jnp.int32, piece.shape, 0)
    return jnp.where(ids < live - first, piece.astype(F32), 0.0).astype(BF16)


def multiply_body(parts_in, depth, has_total, late, spot_ref, sizes_ref, inverse_ref, *refs):
    refs = list(refs)
    pieces = [refs.pop(0) for _ in parts_in]
    before_ref = refs.pop(0) if has_total else None
    total_ref = refs.pop(0)
    later_ref = refs.pop(0) if late else None
    left, right, sem = refs
    share = depth * PARTS
    offsets = [offset for offset, part in parts_in if part == 0]
    copies, firsts = [], []
    for i, offset in enumerate(offsets + [4] * late):
        firsts.append(pl.multiple_of(source_row(spot_ref, offset) * share, share))
        columns = inverse_ref.at[:, pl.ds(firsts[i], share)]
        out = later_ref if i == len(offsets) else left.at[:, i * share : (i + 1) * share]
        copies.append(pltpu.make_async_copy(columns, out, sem.at[i]))
        copies[i].start()
    live = sizes_ref[spot_ref[1]]
    for (offset, part), piece in zip(parts_in, pieces):
        i = offsets.index(offset)
        start = i * share + part * depth
        rows = live_rows(piece[:depth], firsts[i] + part * depth, live)
        right[start : start + depth] = rows
    total = before_ref[...] if has_total else None
    for i in range(len(offsets)):
        copies[i].wait()
        place = slice(i * share, (i + 1) * share)
        part = jnp.dot(left[:, place], right[place], preferred_element_type=F32)
        total = part if total is None else total + part
    total_ref[...] = total
    if late:
        copies[-1].wait()


def multiply(spot, sizes, inverse, depth, named, total=None, late=False):
    parts_in = tuple(n[:2] for n in named)
    pieces = [n[2] for n in named]
    extra = [] if total is None else [total]
    rows, cols = inverse.shape[0], pieces[0].shape[1]
    share = depth * PARTS
    width = depth * len(named)
    out_shape = [jax.ShapeDtypeStruct((rows, cols), F32)]
    if late:
        out_shape.append(jax.ShapeDtypeStruct((rows, share), BF16))
    inverse = pltpu.with_memory_space_constraint(inverse, pltpu.HBM)
    return pl.pallas_call(
        functools.partial(multiply_body, parts_in, depth, bool(extra), late),
        out_shape=out_shape,
        in_specs=[SMEM, SMEM, HBM] + [VMEM] * (len(pieces) + len(extra)),
        out_specs=[VMEM] * len(out_shape),
        scratch_shapes=[
            pltpu.VMEM((rows, width), BF16),
            pltpu.VMEM((width, cols), BF16),
            pltpu.SemaphoreType.DMA((width // share + late,)),
        ],
        compiler_params=params(),
        cost_estimate=pl.CostEstimate(
            flops=2 * rows * width * cols, bytes_accessed=2 * rows * width, transcendentals=0
        ),
    )(spot, sizes, inverse, *pieces, *extra)


def contribute_body(spot_ref, sizes_ref, total_ref, later_ref, lower_ref, *refs):
    pieces, carriers, outs = refs[:PARTS], refs[PARTS:-9], refs[-9:-3]
    top_ref, right, product_ref = refs[-3:]
    live, row = sizes_ref[spot_ref[1]], spot_ref[0]
    depth = later_ref.shape[1] // PARTS
    for k, carrier in enumerate((*carriers, pieces[0])):
        top_ref[k] = carrier[depth:]
    first = source_row(spot_ref, 4) * PARTS * depth
    for part, piece in enumerate(pieces):
        place = part * depth
        right[place : place + depth] = live_rows(piece[:depth], first + place, live)
    total = total_ref[...] + jnp.dot(later_ref[...], right[...], preferred_element_type=F32)
    solved = live_rows(total, row * total.shape[0], live)
    product_ref[...] = jnp.dot(lower_ref[...], solved, preferred_element_type=F32)
    z, y = row // 2, row & 1
    slabs, height, _ = outs[0].shape
    for k in range(4):
        for j in range(slabs):
            base = j * BLOCK + (z ^ k) * 2 * height
            mine = pl.multiple_of(base + y * height, height)
            other = pl.multiple_of(base + (1 - y) * height, height)
            outs[k][j] = product_ref[pl.ds(mine, height)]
            sent = product_ref[pl.ds(other, height)].astype(BF16)
            outs[4 + k // 2][k % 2 * slabs + j] = sent


def contribute(spot, sizes, total, later, lower, pieces, carriers):
    border, rows = lower.shape
    cols = total.shape[1]
    slot = (border // BLOCK, BLOCK // 8, cols)
    count = len(carriers) + 1
    tops = (count, pieces[0].shape[0] - later.shape[1] // PARTS, cols)
    out = pl.pallas_call(
        contribute_body,
        out_shape=[jax.ShapeDtypeStruct(slot, F32)] * 4
        + [jax.ShapeDtypeStruct((2 * slot[0],) + slot[1:], BF16)] * 2
        + [jax.ShapeDtypeStruct(tops, BF16)],
        in_specs=[SMEM, SMEM] + [VMEM] * (3 + len(pieces) + len(carriers)),
        out_specs=[VMEM] * 7,
        scratch_shapes=[
            pltpu.VMEM((later.shape[1], cols), BF16),
            pltpu.VMEM((border, cols), F32),
        ],
        compiler_params=params(),
        cost_estimate=pl.CostEstimate(
            flops=2 * rows * cols * (later.shape[1] + border),
            bytes_accessed=2 * rows * (later.shape[1] + border),
            transcendentals=0,
        ),
    )(spot, sizes, total, later, lower, *pieces, *carriers)
    return out[:4], out[4:6], out[6]


def place_body(targets_ref, spot_ref, *refs):
    pieces, slots_ref, total_ref = refs[:4], refs[4], refs[5]
    total_ref[...] = jnp.zeros_like(total_ref)
    blocks = slots_ref.shape[0]
    slabs = pieces[0].shape[0]
    group = spot_ref[1]
    first = group * blocks
    for k, piece in enumerate(pieces):
        for j in range(slabs):
            place = targets_ref[group ^ k, j] - first

            place = jnp.where((place >= 0) & (place < blocks), place, blocks)
            total_ref[place] += piece[j].astype(F32)

    slots_ref[...] = total_ref[:blocks].astype(BF16)


def place(targets, spot, pieces, blocks):
    shape = (blocks,) + pieces[0].shape[1:]
    return pl.pallas_call(
        place_body,
        out_shape=jax.ShapeDtypeStruct(shape, BF16),
        in_specs=[pl.BlockSpec(memory_space=pltpu.SMEM)] * 2
        + [pl.BlockSpec(memory_space=pltpu.VMEM)] * 4,
        out_specs=pl.BlockSpec(memory_space=pltpu.VMEM),
        scratch_shapes=[pltpu.VMEM((blocks + 1,) + shape[1:], F32)],
        compiler_params=params(),
    )(targets, spot, *pieces)


def reorder_body(spot_ref, order_ref, inverse_ref, *out_refs):
    row, core = spot_ref[0], spot_ref[1] & 1
    half, width = inverse_ref.shape[0] // 2, inverse_ref.shape[1]
    rows = (row * 2 + core) * half + lax.broadcasted_iota(jnp.int32, (half, width), 0)
    cols = lax.broadcasted_iota(jnp.int32, (half, width), 1)
    mine = inverse_ref[pl.ds(pl.multiple_of(core * half, half), half)].astype(F32)
    lower = jnp.where(cols < rows, mine, jnp.where(cols == rows, 1.0, 0.0)).astype(BF16)
    for side, out_ref in ((core, out_refs[0]), (1 - core, out_refs[1])):
        picks = []
        for offset in ORDER:
            first = (source_row(spot_ref, offset) * 2 + side) * half
            ids = first + lax.broadcasted_iota(jnp.int32, (half, width), 0)
            picks.append((ids == order_ref[...]).astype(F32).astype(BF16))
        pick = jnp.concatenate(picks)
        moved = lax.dot_general(
            lower, pick, (((1,), (1,)), ((), ())), preferred_element_type=F32
        )
        out_ref[...] = moved.astype(BF16)


def reorder(spot, order, inverse):
    half, width = inverse.shape[0] // 2, inverse.shape[1]
    return pl.pallas_call(
        reorder_body,
        out_shape=[jax.ShapeDtypeStruct((half, width // 2), BF16)] * 2,
        in_specs=[SMEM, VMEM, VMEM],
        out_specs=[VMEM, VMEM],
        compiler_params=params(),
    )(spot, order[None], inverse)


def factor_body(mine_ref, other_ref, top_ref, came_ref, slots_ref, out_ref):
    count, half, cols = top_ref.shape
    slots = slots_ref.shape[0]
    total = jnp.dot(
        mine_ref[...], top_ref[...].reshape(count * half, cols), preferred_element_type=F32
    ) + jnp.dot(
        other_ref[...], came_ref[...].reshape(count * half, cols), preferred_element_type=F32
    )
    out_ref[:slots] = slots_ref[...]
    out_ref[slots:] = total.astype(BF16).reshape(out_ref.shape[0] - slots, -1, cols)


def panel_factor(mine, other, top, came, slots):
    count, height, cols = slots.shape
    return pl.pallas_call(
        factor_body,
        out_shape=jax.ShapeDtypeStruct((count + mine.shape[0] // height, height, cols), BF16),
        in_specs=[VMEM] * 5,
        out_specs=VMEM,
        compiler_params=params(),
    )(mine, other, top, came, slots)


def base_body(place_ref, surface_ref, lower_ref, mine_ref, other_ref, out_ref, factor_ref):
    row, core = place_ref[0], place_ref[1] & 1
    half = mine_ref.shape[1]
    for ref, side in ((mine_ref, core), (other_ref, 1 - core)):
        for k, apart in enumerate((0, 1, 4, 5, 2, 3, 6, 7)):
            first = pl.multiple_of(((row ^ apart) * 2 + side) * half, half)
            factor_ref[pl.ds(first, half)] = ref[k]
    product = jnp.dot(lower_ref[...], factor_ref[...], preferred_element_type=F32)
    out_ref[...] = surface_ref[...] - product


def panel_update(place_scalars, surface, lower, mine, other):
    return pl.pallas_call(
        base_body,
        out_shape=jax.ShapeDtypeStruct(surface.shape, F32),
        in_specs=[pl.BlockSpec(memory_space=pltpu.SMEM)]
        + [pl.BlockSpec(memory_space=pltpu.VMEM)] * 4,
        out_specs=pl.BlockSpec(memory_space=pltpu.VMEM),
        scratch_shapes=[pltpu.VMEM((lower.shape[1], surface.shape[1]), BF16)],
        compiler_params=params(),
    )(place_scalars, surface, lower, mine, other)


def staged(
    surface,
    panel_lower,
    top_rows,
    panel_inverse,
    panel_order,
    front_inverse,
    front_upper,
    front_lower,
    front_sizes,
    border_blocks,
):
    row_count = lax.axis_size("row")
    group = lax.axis_index("grp")
    row = lax.axis_index("row")
    core = group % 2
    inverse, upper, lower = front_inverse[0], front_upper[0], front_lower[0]
    spot = jnp.stack([row, group])
    inverse = pltpu.with_memory_space_constraint(inverse, pltpu.HBM)
    depth = upper.shape[0] // PARTS

    half = top_rows.shape[0] // 2
    top = lax.dynamic_slice_in_dim(top_rows, core * half, half, 0)
    a, b = jnp.concatenate([upper[:depth], top]), upper[depth:]

    fold = functools.partial(multiply, spot, front_sizes, inverse, depth)
    a_up, a_down, b_up, b_down = ring_send(a, 1), ring_send(a, -1), ring_send(b, 1), ring_send(b, -1)
    lower_mine, lower_other = reorder(spot, panel_order, panel_inverse)
    a_up, a_down, lower_mine = together((a_up, a_down, lower_mine))
    a_up2, a_down2 = ring_send(a_up, 1), ring_send(a_down, -1)
    b_up, b_down = together((b_up, b_down))
    b_up2, b_down2 = ring_send(b_up, 1), ring_send(b_down, -1)
    named = [(0, 0, a), (0, 1, b), (-1, 0, a_up), (-1, 1, b_up), (1, 0, a_down), (1, 1, b_down)]
    (total,) = fold(named)
    a_up2, a_down2, total = together((a_up2, a_down2, total))
    a_up3, a_down3 = ring_send(a_up2, 1), ring_send(a_down2, -1)
    b_up2, b_down2 = together((b_up2, b_down2))
    b_up3, b_down3 = ring_send(b_up2, 1), ring_send(b_down2, -1)
    named = [(-2, 0, a_up2), (-2, 1, b_up2), (2, 0, a_down2), (2, 1, b_down2)]
    (total,) = fold(named, total)
    a_up3, a_down3, total = together((a_up3, a_down3, total))
    a4 = ring_send(a_up3, 1)
    b_up3, b_down3 = together((b_up3, b_down3))
    b4 = ring_send(b_down3, -1)
    named = [(-3, 0, a_up3), (-3, 1, b_up3), (3, 0, a_down3), (3, 1, b_down3)]
    total, later = fold(named, total, late=True)
    carriers = (a, a_up, a_down, a_up2, a_down2, a_up3, a_down3)
    keep, send, top_mine = contribute(
        spot, front_sizes, total, later, lower, (a4, b4), carriers
    )

    top_other = group_swap(top_mine, 1)
    come32 = across(send[1])
    last = panel_factor(lower_mine, lower_other, top_mine, top_other, send[0])
    come10 = across(last)
    come32, last = together((come32, last))
    slabs = keep[0].shape[0]
    come = [come10[:slabs], come10[slabs : 2 * slabs], come32[:slabs], come32[slabs:]]
    sums = [keep[k] + come[k].astype(F32) for k in range(4)]
    swapped = {k: along(sums[k].astype(BF16), k) for k in (3, 2, 1)}
    factor = jnp.stack([last[2 * slabs :], come10[2 * slabs :]])
    swapped[2], factor = together((swapped[2], factor))
    factor_in = along(factor, 2)
    mine = sums[0] + swapped[1].astype(F32) + swapped[2].astype(F32) + swapped[3].astype(F32)
    mine = mine.astype(BF16)
    pieces = [mine] + [group_swap(mine, k) for k in (1, 2, 3)]
    pieces[1], factor_in = together((pieces[1], factor_in))
    factor4 = jnp.concatenate([factor, factor_in])
    factor_mine = jnp.concatenate([factor4, along(factor4, 1)])
    factor_mine = factor_mine.reshape((row_count, half) + top.shape[1:])
    factor_other = group_swap(factor_mine, 1)
    base = panel_update(spot, surface, panel_lower, factor_mine, factor_other)
    local_blocks = surface.shape[0] // BLOCK
    blocks = local_blocks * row_count
    slots = place(border_blocks, spot, pieces, blocks)
    slots = slots.reshape((row_count, local_blocks) + slots.shape[1:])
    got = lax.all_to_all(slots, "row", 0, 0, tiled=True)
    collected = got.transpose(1, 0, 2, 3).reshape(surface.shape).astype(F32)
    return base - collected


def gathered(
    surface,
    panel_lower,
    top_rows,
    panel_inverse,
    panel_order,
    front_inverse,
    front_upper,
    front_lower,
    front_sizes,
    border_blocks,
):
    row_count = lax.axis_size("row")
    grp_index = lax.axis_index("grp")
    row_index = lax.axis_index("row")
    inverse_rows, upper_local, lower_local = front_inverse[0], front_upper[0], front_lower[0]
    local_piv, col_count = upper_local.shape
    pivot_ids = row_index * local_piv + jnp.arange(local_piv, dtype=jnp.int32)
    live_mask = pivot_ids < front_sizes[grp_index]
    upper_kept = jnp.where(live_mask[:, None], upper_local, jnp.zeros_like(upper_local))
    lower_kept = jnp.where(live_mask[None, :], lower_local, jnp.zeros_like(lower_local))
    upper_all = lax.all_gather(upper_kept, "row", axis=0, tiled=True)
    solved = jnp.dot(inverse_rows, upper_all, preferred_element_type=F32).astype(BF16)
    partial_sum = jnp.dot(lower_kept, solved, preferred_element_type=F32)
    own_share = lax.psum_scatter(partial_sum, "row", scatter_dimension=0, tiled=True)
    contributions = lax.all_gather(own_share, ("grp", "row"), axis=0, tiled=True)
    local_blocks = surface.shape[0] // BLOCK
    device_id = grp_index * row_count + row_index
    own_ids = device_id * local_blocks + jnp.arange(local_blocks, dtype=jnp.int32)
    targets = border_blocks.reshape(-1)
    selector = (own_ids[:, None] == targets[None, :]).astype(F32)
    slabs = contributions.reshape(targets.shape[0], BLOCK * col_count)
    collected = jnp.dot(
        selector, slabs, precision=lax.Precision.HIGHEST, preferred_element_type=F32
    ).reshape(surface.shape)
    local_panel, panel_width = panel_inverse.shape
    panel_ids = jnp.arange(panel_width, dtype=jnp.int32)
    top_all = lax.all_gather(top_rows, "row", axis=0, tiled=True)
    ordered = jnp.take(top_all, panel_order, axis=0)
    own_rows = row_index * local_panel + jnp.arange(local_panel, dtype=jnp.int32)
    strict = jnp.where(
        panel_ids[None, :] < own_rows[:, None], panel_inverse, jnp.zeros_like(panel_inverse)
    )
    own_top = lax.dynamic_slice_in_dim(ordered, row_index * local_panel, local_panel, 0)
    product = jnp.dot(strict, ordered, preferred_element_type=F32)
    own_solved = (product + own_top.astype(F32)).astype(BF16)
    factor = lax.all_gather(own_solved, "row", axis=0, tiled=True)
    return surface - collected - jnp.dot(panel_lower, factor, preferred_element_type=F32)


def solution(mesh):
    in_specs = (
        P(("grp", "row"), None),
        P(("grp", "row"), None),
        P("row", None),
        P("row", None),
        P(),
        P("grp", "row", None),
        P("grp", "row", None),
        P("grp", None, "row"),
        P(),
        P(),
    )
    out_specs = P(("grp", "row"), None)
    small = mesh.shape["row"] == 8 and mesh.shape["grp"] == 4
    return jax.shard_map(
        staged if small else gathered,
        mesh=mesh,
        in_specs=in_specs,
        out_specs=out_specs,
        check_vma=False,
    )
```

```python
import functools

import jax
import jax.numpy as jnp
from jax import lax
from jax.experimental import pallas as pl
from jax.experimental.pallas import tpu as pltpu
from jax.sharding import PartitionSpec as P

BLOCK = 128
PARTS = 2
ORDER = (0, -1, 1, -2, 2, -3, 3, 4)
LIMIT = 20 << 20
F32 = jnp.float32
BF16 = jnp.bfloat16
together = lax.optimization_barrier


def params():
    return pltpu.CompilerParams(vmem_limit_bytes=LIMIT)


def row_permute(value, target):
    pairs = [(z * 2 + y, target(z, y)) for z in range(4) for y in range(2)]
    return lax.ppermute(value, "row", [(s, t[0] * 2 + t[1]) for s, t in pairs])


def ring_place(row):
    z, y = row // 2, row & 1
    return z + y * (7 - 2 * z)


def ring_row(place):
    y = place >> 2
    return (place + y * (7 - 2 * place)) * 2 + y


def ring_send(value, step):
    pairs = [(r, ring_row((ring_place(r) + step) & 7)) for r in range(8)]
    return lax.ppermute(value, "row", pairs)


def across(value):
    return row_permute(value, lambda z, y: (z, 1 - y))


def along(value, step):
    return row_permute(value, lambda z, y: (z ^ step, y))


def group_swap(value, step):
    return lax.ppermute(value, "grp", [(g, g ^ step) for g in range(4)])


SMEM = pl.BlockSpec(memory_space=pltpu.SMEM)
VMEM = pl.BlockSpec(memory_space=pltpu.VMEM)
HBM = pl.BlockSpec(memory_space=pltpu.HBM)


def source_row(spot_ref, offset):
    return ring_row((ring_place(spot_ref[0]) + offset) & 7)


def live_rows(piece, first, live):
    ids = lax.broadcasted_iota(jnp.int32, piece.shape, 0)
    return jnp.where(ids < live - first, piece.astype(F32), 0.0).astype(BF16)


def multiply_body(parts_in, depth, has_total, late, spot_ref, sizes_ref, inverse_ref, *refs):
    refs = list(refs)
    pieces = [refs.pop(0) for _ in parts_in]
    before_ref = refs.pop(0) if has_total else None
    total_ref = refs.pop(0)
    later_ref = refs.pop(0) if late else None
    left, right, sem = refs
    share = depth * PARTS
    offsets = [offset for offset, part in parts_in if part == 0]
    copies, firsts = [], []
    for i, offset in enumerate(offsets + [4] * late):
        firsts.append(pl.multiple_of(source_row(spot_ref, offset) * share, share))
        columns = inverse_ref.at[:, pl.ds(firsts[i], share)]
        out = later_ref if i == len(offsets) else left.at[:, i * share : (i + 1) * share]
        copies.append(pltpu.make_async_copy(columns, out, sem.at[i]))
        copies[i].start()
    live = sizes_ref[spot_ref[1]]
    for (offset, part), piece in zip(parts_in, pieces):
        i = offsets.index(offset)
        start = i * share + part * depth
        rows = live_rows(piece[:depth], firsts[i] + part * depth, live)
        right[start : start + depth] = rows
    total = before_ref[...] if has_total else None
    for i in range(len(offsets)):
        copies[i].wait()
        place = slice(i * share, (i + 1) * share)
        part = jnp.dot(left[:, place], right[place], preferred_element_type=F32)
        total = part if total is None else total + part
    total_ref[...] = total
    if late:
        copies[-1].wait()


def multiply(spot, sizes, inverse, depth, named, total=None, late=False):
    parts_in = tuple(n[:2] for n in named)
    pieces = [n[2] for n in named]
    extra = [] if total is None else [total]
    rows, cols = inverse.shape[0], pieces[0].shape[1]
    share = depth * PARTS
    width = depth * len(named)
    out_shape = [jax.ShapeDtypeStruct((rows, cols), F32)]
    if late:
        out_shape.append(jax.ShapeDtypeStruct((rows, share), BF16))
    inverse = pltpu.with_memory_space_constraint(inverse, pltpu.HBM)
    return pl.pallas_call(
        functools.partial(multiply_body, parts_in, depth, bool(extra), late),
        out_shape=out_shape,
        in_specs=[SMEM, SMEM, HBM] + [VMEM] * (len(pieces) + len(extra)),
        out_specs=[VMEM] * len(out_shape),
        scratch_shapes=[
            pltpu.VMEM((rows, width), BF16),
            pltpu.VMEM((width, cols), BF16),
            pltpu.SemaphoreType.DMA((width // share + late,)),
        ],
        compiler_params=params(),
        cost_estimate=pl.CostEstimate(
            flops=2 * rows * width * cols, bytes_accessed=2 * rows * width, transcendentals=0
        ),
    )(spot, sizes, inverse, *pieces, *extra)


def contribute_body(spot_ref, sizes_ref, total_ref, later_ref, lower_ref, *refs):
    pieces, carriers, outs = refs[:PARTS], refs[PARTS:-9], refs[-9:-3]
    top_ref, right, product_ref = refs[-3:]
    live, row = sizes_ref[spot_ref[1]], spot_ref[0]
    depth = later_ref.shape[1] // PARTS
    for k, carrier in enumerate((*carriers, pieces[0])):
        top_ref[k] = carrier[depth:]
    first = source_row(spot_ref, 4) * PARTS * depth
    for part, piece in enumerate(pieces):
        place = part * depth
        right[place : place + depth] = live_rows(piece[:depth], first + place, live)
    total = total_ref[...] + jnp.dot(later_ref[...], right[...], preferred_element_type=F32)
    solved = live_rows(total, row * total.shape[0], live)
    product_ref[...] = jnp.dot(lower_ref[...], solved, preferred_element_type=F32)
    z, y = row // 2, row & 1
    slabs, height, _ = outs[0].shape
    for k in range(4):
        for j in range(slabs):
            base = j * BLOCK + (z ^ k) * 2 * height
            mine = pl.multiple_of(base + y * height, height)
            other = pl.multiple_of(base + (1 - y) * height, height)
            outs[k][j] = product_ref[pl.ds(mine, height)]
            sent = product_ref[pl.ds(other, height)].astype(BF16)
            outs[4 + k // 2][k % 2 * slabs + j] = sent


def contribute(spot, sizes, total, later, lower, pieces, carriers):
    border, rows = lower.shape
    cols = total.shape[1]
    slot = (border // BLOCK, BLOCK // 8, cols)
    count = len(carriers) + 1
    tops = (count, pieces[0].shape[0] - later.shape[1] // PARTS, cols)
    out = pl.pallas_call(
        contribute_body,
        out_shape=[jax.ShapeDtypeStruct(slot, F32)] * 4
        + [jax.ShapeDtypeStruct((2 * slot[0],) + slot[1:], BF16)] * 2
        + [jax.ShapeDtypeStruct(tops, BF16)],
        in_specs=[SMEM, SMEM] + [VMEM] * (3 + len(pieces) + len(carriers)),
        out_specs=[VMEM] * 7,
        scratch_shapes=[
            pltpu.VMEM((later.shape[1], cols), BF16),
            pltpu.VMEM((border, cols), F32),
        ],
        compiler_params=params(),
        cost_estimate=pl.CostEstimate(
            flops=2 * rows * cols * (later.shape[1] + border),
            bytes_accessed=2 * rows * (later.shape[1] + border),
            transcendentals=0,
        ),
    )(spot, sizes, total, later, lower, *pieces, *carriers)
    return out[:4], out[4:6], out[6]


def place_body(targets_ref, *refs):
    pieces, slots_ref, total_ref = refs[:4], refs[4], refs[5]
    total_ref[...] = jnp.zeros_like(total_ref)
    blocks = slots_ref.shape[0]
    for k, piece in enumerate(pieces):
        for j in range(piece.shape[0]):
            total_ref[targets_ref[k, j]] += piece[j].astype(F32)
    slots_ref[...] = total_ref[:blocks].astype(BF16)


def place(targets, group, pieces, blocks):
    shape = (blocks,) + pieces[0].shape[1:]
    fronts = group ^ jnp.arange(len(pieces), dtype=jnp.int32)
    at = jnp.take(targets, fronts, axis=0) - group * blocks
    at = jnp.where((at >= 0) & (at < blocks), at, blocks)
    return pl.pallas_call(
        place_body,
        out_shape=jax.ShapeDtypeStruct(shape, BF16),
        in_specs=[SMEM] + [VMEM] * 4,
        out_specs=VMEM,
        scratch_shapes=[pltpu.VMEM((blocks + 1,) + shape[1:], F32)],
        compiler_params=params(),
    )(at, *pieces)


def reorder_body(spot_ref, order_ref, inverse_ref, *out_refs):
    row, core = spot_ref[0], spot_ref[1] & 1
    half, width = inverse_ref.shape[0] // 2, inverse_ref.shape[1]
    rows = (row * 2 + core) * half + lax.broadcasted_iota(jnp.int32, (half, width), 0)
    cols = lax.broadcasted_iota(jnp.int32, (half, width), 1)
    mine = inverse_ref[pl.ds(pl.multiple_of(core * half, half), half)].astype(F32)
    lower = jnp.where(cols < rows, mine, jnp.where(cols == rows, 1.0, 0.0)).astype(BF16)
    for side, out_ref in ((core, out_refs[0]), (1 - core, out_refs[1])):
        picks = []
        for offset in ORDER:
            first = (source_row(spot_ref, offset) * 2 + side) * half
            ids = first + lax.broadcasted_iota(jnp.int32, (half, width), 0)
            picks.append((ids == order_ref[...]).astype(F32).astype(BF16))
        pick = jnp.concatenate(picks)
        moved = lax.dot_general(
            lower, pick, (((1,), (1,)), ((), ())), preferred_element_type=F32
        )
        out_ref[...] = moved.astype(BF16)


def reorder(spot, order, inverse):
    half, width = inverse.shape[0] // 2, inverse.shape[1]
    return pl.pallas_call(
        reorder_body,
        out_shape=[jax.ShapeDtypeStruct((half, width // 2), BF16)] * 2,
        in_specs=[SMEM, VMEM, VMEM],
        out_specs=[VMEM, VMEM],
        compiler_params=params(),
    )(spot, order[None], inverse)


def factor_body(mine_ref, other_ref, top_ref, came_ref, slots_ref, out_ref):
    count, half, cols = top_ref.shape
    slots = slots_ref.shape[0]
    total = jnp.dot(
        mine_ref[...], top_ref[...].reshape(count * half, cols), preferred_element_type=F32
    ) + jnp.dot(
        other_ref[...], came_ref[...].reshape(count * half, cols), preferred_element_type=F32
    )
    out_ref[:slots] = slots_ref[...]
    out_ref[slots:] = total.astype(BF16).reshape(out_ref.shape[0] - slots, -1, cols)


def panel_factor(mine, other, top, came, slots):
    count, height, cols = slots.shape
    return pl.pallas_call(
        factor_body,
        out_shape=jax.ShapeDtypeStruct((count + mine.shape[0] // height, height, cols), BF16),
        in_specs=[VMEM] * 5,
        out_specs=VMEM,
        compiler_params=params(),
    )(mine, other, top, came, slots)


def base_body(place_ref, surface_ref, lower_ref, mine_ref, other_ref, out_ref, factor_ref):
    row, core = place_ref[0], place_ref[1] & 1
    half = mine_ref.shape[1]
    for ref, side in ((mine_ref, core), (other_ref, 1 - core)):
        for k, apart in enumerate((0, 1, 4, 5, 2, 3, 6, 7)):
            first = pl.multiple_of(((row ^ apart) * 2 + side) * half, half)
            factor_ref[pl.ds(first, half)] = ref[k]
    product = jnp.dot(lower_ref[...], factor_ref[...], preferred_element_type=F32)
    out_ref[...] = surface_ref[...] - product


def panel_update(place_scalars, surface, lower, mine, other):
    return pl.pallas_call(
        base_body,
        out_shape=jax.ShapeDtypeStruct(surface.shape, F32),
        in_specs=[pl.BlockSpec(memory_space=pltpu.SMEM)]
        + [pl.BlockSpec(memory_space=pltpu.VMEM)] * 4,
        out_specs=pl.BlockSpec(memory_space=pltpu.VMEM),
        scratch_shapes=[pltpu.VMEM((lower.shape[1], surface.shape[1]), BF16)],
        compiler_params=params(),
    )(place_scalars, surface, lower, mine, other)


def staged(
    surface,
    panel_lower,
    top_rows,
    panel_inverse,
    panel_order,
    front_inverse,
    front_upper,
    front_lower,
    front_sizes,
    border_blocks,
):
    row_count = lax.axis_size("row")
    group = lax.axis_index("grp")
    row = lax.axis_index("row")
    core = group % 2
    inverse, upper, lower = front_inverse[0], front_upper[0], front_lower[0]
    spot = jnp.stack([row, group])
    inverse = pltpu.with_memory_space_constraint(inverse, pltpu.HBM)
    depth = upper.shape[0] // PARTS

    half = top_rows.shape[0] // 2
    top = lax.dynamic_slice_in_dim(top_rows, core * half, half, 0)
    a, b = jnp.concatenate([upper[:depth], top]), upper[depth:]

    fold = functools.partial(multiply, spot, front_sizes, inverse, depth)
    a_up, a_down, b_up, b_down = ring_send(a, 1), ring_send(a, -1), ring_send(b, 1), ring_send(b, -1)
    lower_mine, lower_other = reorder(spot, panel_order, panel_inverse)
    a_up, a_down, lower_mine = together((a_up, a_down, lower_mine))
    a_up2, a_down2 = ring_send(a_up, 1), ring_send(a_down, -1)
    b_up, b_down = together((b_up, b_down))
    b_up2, b_down2 = ring_send(b_up, 1), ring_send(b_down, -1)
    named = [(0, 0, a), (0, 1, b), (-1, 0, a_up), (-1, 1, b_up), (1, 0, a_down), (1, 1, b_down)]
    (total,) = fold(named)
    a_up2, a_down2, total = together((a_up2, a_down2, total))
    a_up3, a_down3 = ring_send(a_up2, 1), ring_send(a_down2, -1)
    b_up2, b_down2 = together((b_up2, b_down2))
    b_up3, b_down3 = ring_send(b_up2, 1), ring_send(b_down2, -1)
    named = [(-2, 0, a_up2), (-2, 1, b_up2), (2, 0, a_down2), (2, 1, b_down2)]
    (total,) = fold(named, total)
    a_up3, a_down3, total = together((a_up3, a_down3, total))
    a4 = ring_send(a_up3, 1)
    b_up3, b_down3 = together((b_up3, b_down3))
    b4 = ring_send(b_down3, -1)
    named = [(-3, 0, a_up3), (-3, 1, b_up3), (3, 0, a_down3), (3, 1, b_down3)]
    total, later = fold(named, total, late=True)
    carriers = (a, a_up, a_down, a_up2, a_down2, a_up3, a_down3)
    keep, send, top_mine = contribute(
        spot, front_sizes, total, later, lower, (a4, b4), carriers
    )

    top_other = group_swap(top_mine, 1)
    come32 = across(send[1])
    last = panel_factor(lower_mine, lower_other, top_mine, top_other, send[0])
    come10 = across(last)
    come32, last = together((come32, last))
    slabs = keep[0].shape[0]
    come = [come10[:slabs], come10[slabs : 2 * slabs], come32[:slabs], come32[slabs:]]
    sums = [keep[k] + come[k].astype(F32) for k in range(4)]
    swapped = {k: along(sums[k].astype(BF16), k) for k in (3, 2, 1)}
    factor = jnp.stack([last[2 * slabs :], come10[2 * slabs :]])
    swapped[2], factor = together((swapped[2], factor))
    factor_in = along(factor, 2)
    mine = sums[0] + swapped[1].astype(F32) + swapped[2].astype(F32) + swapped[3].astype(F32)
    mine = mine.astype(BF16)
    pieces = [mine] + [group_swap(mine, k) for k in (1, 2, 3)]
    pieces[1], factor_in = together((pieces[1], factor_in))
    factor4 = jnp.concatenate([factor, factor_in])
    factor_mine = jnp.concatenate([factor4, along(factor4, 1)])
    factor_mine = factor_mine.reshape((row_count, half) + top.shape[1:])
    factor_other = group_swap(factor_mine, 1)
    base = panel_update(spot, surface, panel_lower, factor_mine, factor_other)
    local_blocks = surface.shape[0] // BLOCK
    blocks = local_blocks * row_count
    slots = place(border_blocks, group, pieces, blocks)
    slots = slots.reshape((row_count, local_blocks) + slots.shape[1:])
    got = lax.all_to_all(slots, "row", 0, 0, tiled=True)
    collected = got.transpose(1, 0, 2, 3).reshape(surface.shape).astype(F32)
    return base - collected


def gathered(
    surface,
    panel_lower,
    top_rows,
    panel_inverse,
    panel_order,
    front_inverse,
    front_upper,
    front_lower,
    front_sizes,
    border_blocks,
):
    row_count = lax.axis_size("row")
    grp_index = lax.axis_index("grp")
    row_index = lax.axis_index("row")
    inverse_rows, upper_local, lower_local = front_inverse[0], front_upper[0], front_lower[0]
    local_piv, col_count = upper_local.shape
    pivot_ids = row_index * local_piv + jnp.arange(local_piv, dtype=jnp.int32)
    live_mask = pivot_ids < front_sizes[grp_index]
    upper_kept = jnp.where(live_mask[:, None], upper_local, jnp.zeros_like(upper_local))
    lower_kept = jnp.where(live_mask[None, :], lower_local, jnp.zeros_like(lower_local))
    upper_all = lax.all_gather(upper_kept, "row", axis=0, tiled=True)
    solved = jnp.dot(inverse_rows, upper_all, preferred_element_type=F32).astype(BF16)
    partial_sum = jnp.dot(lower_kept, solved, preferred_element_type=F32)
    own_share = lax.psum_scatter(partial_sum, "row", scatter_dimension=0, tiled=True)
    contributions = lax.all_gather(own_share, ("grp", "row"), axis=0, tiled=True)
    local_blocks = surface.shape[0] // BLOCK
    device_id = grp_index * row_count + row_index
    own_ids = device_id * local_blocks + jnp.arange(local_blocks, dtype=jnp.int32)
    targets = border_blocks.reshape(-1)
    selector = (own_ids[:, None] == targets[None, :]).astype(F32)
    slabs = contributions.reshape(targets.shape[0], BLOCK * col_count)
    collected = jnp.dot(
        selector, slabs, precision=lax.Precision.HIGHEST, preferred_element_type=F32
    ).reshape(surface.shape)
    local_panel, panel_width = panel_inverse.shape
    panel_ids = jnp.arange(panel_width, dtype=jnp.int32)
    top_all = lax.all_gather(top_rows, "row", axis=0, tiled=True)
    ordered = jnp.take(top_all, panel_order, axis=0)
    own_rows = row_index * local_panel + jnp.arange(local_panel, dtype=jnp.int32)
    strict = jnp.where(
        panel_ids[None, :] < own_rows[:, None], panel_inverse, jnp.zeros_like(panel_inverse)
    )
    own_top = lax.dynamic_slice_in_dim(ordered, row_index * local_panel, local_panel, 0)
    product = jnp.dot(strict, ordered, preferred_element_type=F32)
    own_solved = (product + own_top.astype(F32)).astype(BF16)
    factor = lax.all_gather(own_solved, "row", axis=0, tiled=True)
    return surface - collected - jnp.dot(panel_lower, factor, preferred_element_type=F32)


def solution(mesh):
    in_specs = (
        P(("grp", "row"), None),
        P(("grp", "row"), None),
        P("row", None),
        P("row", None),
        P(),
        P("grp", "row", None),
        P("grp", "row", None),
        P("grp", None, "row"),
        P(),
        P(),
    )
    out_specs = P(("grp", "row"), None)
    small = mesh.shape["row"] == 8 and mesh.shape["grp"] == 4
    return jax.shard_map(
        staged if small else gathered,
        mesh=mesh,
        in_specs=in_specs,
        out_specs=out_specs,
        check_vma=False,
    )
```
